256 devices in a mesh: dp: 8 (over x, y_lo), tensor: 32 (over y_hi, z, core).
Axes of the slice: x: 4, y: 4 (y_hi: 2, y_lo: 2; y = y_hi * 2 + y_lo), z: 8, core: 2. Of those that a mesh axis runs over, the one named last changes fastest.
Arguments:
- tokens: bfloat16 [4096, 8192], P('dp', 'tensor'), may hold values from -6 to 6
- gate_in: bfloat16 [32, 256, 1024], P('tensor'), may hold values from -0.375 to 0.375
- gate_out: bfloat16 [32, 1024, 1024], P('tensor'), may hold values from -0.1875 to 0.1875
- up_in: bfloat16 [32, 256, 1024], P('tensor'), may hold values from -0.375 to 0.375
- up_out: bfloat16 [32, 1024, 1024], P('tensor'), may hold values from -0.1875 to 0.1875
- down_in: bfloat16 [32, 1024, 1024], P('tensor'), may hold values from -0.1875 to 0.1875
- down_out: bfloat16 [32, 1024, 256], P('tensor'), may hold values from -0.1875 to 0.1875
- cotangent: bfloat16 [4096, 8192], P('dp', 'tensor'), may hold values from -0.75 to 0.75
Outputs:
- output: bfloat16 [4096, 8192], P('dp', 'tensor')
- tokens_grad: bfloat16 [4096, 8192], P('dp', 'tensor')
- gate_in_grad: bfloat16 [32, 256, 1024], P('tensor', None, 'dp')
- gate_out_grad: bfloat16 [32, 1024, 1024], P('tensor', 'dp')
- up_in_grad: bfloat16 [32, 256, 1024], P('tensor', None, 'dp')
- up_out_grad: bfloat16 [32, 1024, 1024], P('tensor', 'dp')
- down_in_grad: bfloat16 [32, 1024, 1024], P('tensor', 'dp')
- down_out_grad: bfloat16 [32, 1024, 256], P('tensor', 'dp')
The draws below stay inside these ranges and needn't reach their ends.
All inputs are finite; a program needn't handle non-finite values.
Results may differ from the reference program's by a relative error of at most 0.019.
Values may be sent and summed in bfloat16 or wider, within the bound.
A program may use at most 128 MiB of HBM per device.

```python
import jax
import jax.numpy as jnp

D = 8192
NBLK = 32
TOK_DEV = 512
TOKENS = 4096
DB = 256
MB = 1024
KW = 32
N_DP = 8


def steps_of(rng, shape, pieces, smallest, top_value):
    def one(axis_at, blocks):
        steps = jax.random.uniform(jax.random.fold_in(jax.random.fold_in(rng, 6), axis_at), (blocks,), jnp.float32, smallest / len(pieces), top_value / len(pieces))
        return jnp.repeat(jnp.exp(steps), shape[axis_at] // blocks).reshape((-1,) + (1,) * (len(shape) - axis_at - 1))

    factor_of = one(*pieces[0])
    for cut in pieces[1:]:
        factor_of = factor_of * one(*cut)
    return factor_of


def gaussian(stream_key, dims, spread, reach, split=(), held_as=jnp.bfloat16):
    array = jax.random.normal(stream_key, dims, jnp.float32) * spread
    if len(split) > 0:
        array = steps_of(stream_key, dims, split, -0.22, 0.18) * array
    return jnp.clip(array, min=-reach, max=reach).astype(held_as)


def setup_inputs(seed: int = 0) -> dict:
    arg_keys = jax.random.split(jax.random.key(seed), 9)
    return {
        "tokens": gaussian(arg_keys[0], (TOKENS, D), 1.0, 6.0, ((0, 8), (1, 32))),
        "gate_in": gaussian(arg_keys[1], (NBLK, DB, MB), DB ** -0.5, 0.375, ((0, 32),)),
        "gate_out": gaussian(arg_keys[2], (NBLK, MB, MB), MB ** -0.5, 0.1875, ((0, 32),)),
        "up_in": gaussian(arg_keys[3], (NBLK, DB, MB), DB ** -0.5, 0.375, ((0, 32),)),
        "up_out": gaussian(arg_keys[4], (NBLK, MB, MB), MB ** -0.5, 0.1875, ((0, 32),)),
        "down_in": gaussian(arg_keys[5], (NBLK, MB, MB), MB ** -0.5, 0.1875, ((0, 32),)),
        "down_out": gaussian(arg_keys[6], (NBLK, MB, DB), MB ** -0.5, 0.1875, ((0, 32),)),
        "cotangent": gaussian(arg_keys[7], (TOKENS, D), 0.125, 0.75, ((0, 8), (1, 32))),
    }


def flt(a):
    return a.astype(jnp.float32)


def reference(tokens, gate_in, gate_out, up_in, up_out, down_in, down_out, cotangent):
    rg = flt(gate_in).reshape(NBLK, DB, NBLK, KW)
    ru = flt(up_in).reshape(NBLK, DB, NBLK, KW)
    lg = flt(gate_out).reshape(NBLK, NBLK, KW, MB)
    lu = flt(up_out).reshape(NBLK, NBLK, KW, MB)
    rd = flt(down_in).reshape(NBLK, MB, NBLK, KW)
    ld = flt(down_out).reshape(NBLK, NBLK, KW, DB)
    outs = []
    dxs = []
    sums = None
    for group in range(N_DP):
        xb = flt(tokens[group * TOK_DEV:(group + 1) * TOK_DEV]).reshape(TOK_DEV, NBLK, DB)
        dyb = flt(cotangent[group * TOK_DEV:(group + 1) * TOK_DEV]).reshape(TOK_DEV, NBLK, DB)
        gmid = jnp.einsum('tbi,bick->cbkt', xb, rg).astype(jnp.bfloat16)
        umid = jnp.einsum('tbi,bick->cbkt', xb, ru).astype(jnp.bfloat16)
        gate = jnp.einsum('cbkt,cbkm->ctm', flt(gmid), lg)
        upper = jnp.einsum('cbkt,cbkm->ctm', flt(umid), lu)
        sig = jax.nn.sigmoid(gate)
        act = gate * sig
        hidden = (act * upper).astype(jnp.bfloat16)
        dmid = jnp.einsum('ctm,cmek->eckt', flt(hidden), rd).astype(jnp.bfloat16)
        outs.append(jnp.einsum('eckt,ecki->tei', flt(dmid), ld).astype(jnp.bfloat16).reshape(TOK_DEV, D))
        ddm = jnp.einsum('tei,ecki->eckt', dyb, ld).astype(jnp.bfloat16)
        g_ld = jnp.einsum('eckt,tei->ecki', flt(dmid), dyb)
        dhid = jnp.einsum('eckt,cmek->ctm', flt(ddm), rd)
        g_rd = jnp.einsum('ctm,eckt->cmek', flt(hidden), flt(ddm))
        dgate = (dhid * upper * sig * (1.0 + gate * (1.0 - sig))).astype(jnp.bfloat16)
        dup = (dhid * act).astype(jnp.bfloat16)
        g_lg = jnp.einsum('cbkt,ctm->cbkm', flt(gmid), flt(dgate))
        g_lu = jnp.einsum('cbkt,ctm->cbkm', flt(umid), flt(dup))
        dgm = jnp.einsum('cbkm,ctm->cbkt', lg, flt(dgate)).astype(jnp.bfloat16)
        dum = jnp.einsum('cbkm,ctm->cbkt', lu, flt(dup)).astype(jnp.bfloat16)
        g_rg = jnp.einsum('tbi,cbkt->bick', xb, flt(dgm))
        g_ru = jnp.einsum('tbi,cbkt->bick', xb, flt(dum))
        dx = jnp.einsum('cbkt,bick->tbi', flt(dgm), rg) + jnp.einsum('cbkt,bick->tbi', flt(dum), ru)
        dxs.append(dx.astype(jnp.bfloat16).reshape(TOK_DEV, D))
        parts = (g_rg.reshape(NBLK, DB, MB), g_lg.reshape(NBLK, MB, MB), g_ru.reshape(NBLK, DB, MB),
                 g_lu.reshape(NBLK, MB, MB), g_rd.reshape(NBLK, MB, MB), g_ld.reshape(NBLK, MB, DB))
        parts = tuple(flt(p.astype(jnp.bfloat16)) for p in parts)
        sums = parts if sums is None else tuple(a + b for a, b in zip(sums, parts))
    grads = tuple(s.astype(jnp.bfloat16) for s in sums)
    return (jnp.concatenate(outs, 0), jnp.concatenate(dxs, 0), grads[0], grads[1], grads[2], grads[3], grads[4], grads[5])
```

```python
import jax
import jax.numpy as jnp
from jax import lax
from jax.experimental import pallas as pl
from jax.experimental.pallas import tpu as pltpu
from jax.sharding import PartitionSpec as P

MESH = pl.DeviceIdType.MESH
BF = jnp.bfloat16
F32 = jnp.float32
NT = (((1,), (1,)), ((), ()))
NN = (((1,), (0,)), ((), ()))
TOK, DB, MB, KW, NBLK, NDP = 512, 256, 1024, 32, 32, 8


def dot(a, b, form=NN):
    return lax.dot_general(a, b, form, preferred_element_type=F32)


def rows_at(index, size):
    return pl.ds(pl.multiple_of(index * size, size), size)


def tiles(count, body):
    def step(i, carry):
        body(i)
        return carry

    lax.fori_loop(0, count, step, 0)


def kernel(
    x_h, rg_h, lg_h, ru_h, lu_h, rd_h, ld_h, dy_h,
    out_o, dx_o, rg_o, lg_o, ru_o, lu_o, rd_o, ld_o,
    x, rg, lg, ru, lu, rd, ld, dy,
    xt, lgt, lut, rdt, ldt,
    send, recv,
    gate, upper, hidden, dgate, dup, dxt,
    p2, pn, pp, ysend, ra, rb, rc, rdn, ye,
    small, rsmall,
    load_sem, a2a_send, a2a_recv, ring_send, ring_recv, small_send, small_recv,
):
    dp, tn = lax.axis_index("dp"), lax.axis_index("tensor")
    xc, yl = dp // 2, dp % 2
    yh, z, core = tn // 16, (tn // 2) % 8, tn % 2

    loads = {}
    for i, (name, src, dst) in enumerate((
        ("x", x_h, x), ("rg", rg_h.at[0], rg), ("ru", ru_h.at[0], ru), ("dy", dy_h, dy), ("ld", ld_h.at[0], ld),
        ("lg", lg_h.at[0], lg), ("lu", lu_h.at[0], lu), ("rd", rd_h.at[0], rd),
    )):
        loads[name] = pltpu.make_async_copy(src, dst, load_sem.at[i])
        loads[name].start()

    def peer(j):
        g = j // 4
        dz = 4 + (1 - 2 * (g % 2)) * ((g + 1) // 2)
        py = (yh + 1 - (j // 2) % 2) % 2
        pz = (z + dz) % 8
        pc = (core + 1 - j % 2) % 2
        return (py * 8 + pz) * 2 + pc

    def dp_peer(j):
        return (dp + 1 + j) % NDP

    barrier = pltpu.get_barrier_semaphore()

    def greet_tensor(j):
        pl.semaphore_signal(barrier, inc=1, device_id=(dp, peer(j)), device_id_type=MESH)

    def greet_dp(j):
        pl.semaphore_signal(barrier, inc=1, device_id=(dp_peer(j), tn), device_id_type=MESH)

    tiles(NBLK - 1, greet_tensor)
    tiles(NDP - 1, greet_dp)

    def exchange(i):
        mine = rows_at(tn, KW)

        def one(j):
            to = peer(j)
            pltpu.make_async_remote_copy(
                src_ref=send.at[i, rows_at(to, KW)], dst_ref=recv.at[i, mine],
                send_sem=a2a_send.at[i], recv_sem=a2a_recv.at[i],
                device_id=(dp, to), device_id_type=MESH,
            ).start()

        tiles(NBLK - 1, one)
        recv[i, mine, :] = send[i, mine, :]

    def await_bytes(ref, sem):
        pltpu.make_async_copy(ref, ref, sem).wait()

    def arrived(i):
        await_bytes(recv.at[i, pl.ds(0, MB - KW)], a2a_recv.at[i])

    GM, UM, DD, DM, DG, DU = range(6)

    def first(i, w):
        def body(q):
            cols = rows_at(q, 256)
            send[i, cols, :] = dot(w[:, cols].T, x[...], NT).astype(BF)

        tiles(4, body)

    loads["x"].wait()
    loads["rg"].wait()
    first(GM, rg)
    pl.semaphore_wait(barrier, NBLK - 1 + NDP - 1)
    exchange(GM)
    loads["ru"].wait()
    first(UM, ru)
    exchange(UM)
    loads["dy"].wait()
    loads["ld"].wait()

    def back_down(q):
        rows = rows_at(q, 256)
        send[DD, rows, :] = dot(ld[rows, :], dy[...], NT).astype(BF)

    tiles(4, back_down)
    exchange(DD)

    def flip(src, dst, across, down):
        def body(i):
            r, c = i // across, i % across
            dst[rows_at(c, 256), rows_at(r, 256)] = src[rows_at(r, 256), rows_at(c, 256)].T

        tiles(across * down, body)

    loads["lg"].wait()
    flip(lg, lgt, 4, 4)
    loads["lu"].wait()
    flip(lu, lut, 4, 4)
    loads["rd"].wait()
    flip(rd, rdt, 4, 4)
    flip(x, xt, 1, 2)
    flip(ld, ldt, 1, 4)

    arrived(GM)
    arrived(UM)

    def forward(q):
        rows = rows_at(q, 256)
        g = dot(lgt[rows, :], recv[GM])
        u = dot(lut[rows, :], recv[UM])
        gate[rows, :] = g
        upper[rows, :] = u
        hidden[rows, :] = (g * jax.nn.sigmoid(g) * u).astype(BF)

    tiles(4, forward)

    def down(q):
        rows = rows_at(q, 256)
        send[DM, rows, :] = dot(rdt[rows, :], hidden[...]).astype(BF)

    tiles(4, down)
    exchange(DM)

    arrived(DD)

    def backward(q):
        rows = rows_at(q, 256)
        dh = dot(rd[rows, :], recv[DD])
        g, u = gate[rows, :], upper[rows, :]
        s = jax.nn.sigmoid(g)
        dgate[rows, :] = (dh * u * s * (1.0 + g * (1.0 - s))).astype(BF)
        dup[rows, :] = (dh * (g * s)).astype(BF)

    tiles(4, backward)

    def mids(i, w, d):
        def body(q):
            rows = rows_at(q, 256)
            send[i, rows, :] = dot(w[rows, :], d[...]).astype(BF)

        tiles(4, body)
        exchange(i)

    mids(DG, lg, dgate)
    mids(DU, lu, dup)

    nxt, prv, opp = (xc + 1) % 4, (xc + 3) % 4, (xc + 2) % 4

    def ship(src, dst, sem, to):
        cp = pltpu.make_async_remote_copy(
            src_ref=src, dst_ref=dst, send_sem=ring_send.at[sem], recv_sem=ring_recv.at[sem],
            device_id=to, device_id_type=MESH,
        )
        cp.start()
        return cp

    to_next, to_prev = (nxt * 2 + yl, tn), (prv * 2 + yl, tn)
    to_pair = (xc * 2 + 1 - yl, tn)
    big = (
        (hidden, recv.at[DD], rd_o),
        (recv.at[GM], dgate, lg_o),
        (recv.at[UM], dup, lu_o),
    )
    ships = []

    def quarter(a, left, right, q, put):
        def body(h):
            rows = pl.ds(pl.multiple_of(q * 256 + h * 128, 128), 128)
            put(h, dot(left[rows, :], right[...], NT))

        tiles(2, body)

    started = [[None] * 5 for _ in big]
    for a, (left, right, _) in enumerate(big):
        def put(h, v, a=a):
            p2[a, h] = v.astype(BF)

        quarter(a, left, right, opp, put)
        started[a][0] = ship(p2.at[a, 0], ra.at[a], 5 * a, to_next)
        started[a][1] = ship(p2.at[a, 1], rb.at[a], 5 * a + 1, to_prev)
    for a, (left, right, _) in enumerate(big):
        def put_n(h, v, a=a):
            pn[a, h] = v.astype(BF)

        def put_p(h, v, a=a):
            pp[a, h] = v.astype(BF)

        quarter(a, left, right, nxt, put_n)
        started[a][0].wait_recv()
        pn[a, 0] = (pn[a, 0].astype(F32) + ra[a].astype(F32)).astype(BF)
        started[a][2] = ship(pn.at[a], rc.at[a], 5 * a + 2, to_next)
        quarter(a, left, right, prv, put_p)
        started[a][1].wait_recv()
        pp[a, 1] = (pp[a, 1].astype(F32) + rb[a].astype(F32)).astype(BF)
        started[a][3] = ship(pp.at[a], rdn.at[a], 5 * a + 3, to_prev)
    for a, (left, right, out) in enumerate(big):
        started[a][2].wait_recv()
        started[a][3].wait_recv()

        def total(h, a=a, left=left, right=right):
            rows = pl.ds(pl.multiple_of(xc * 256 + h * 128, 128), 128)
            return dot(left[rows, :], right[...], NT) + rc[a, h].astype(F32) + rdn[a, h].astype(F32)

        ysend[a] = total(1 - yl).astype(BF)
        started[a][4] = ship(ysend.at[a], ye.at[a], 5 * a + 4, to_pair)
        own = total(yl)
        upper[pl.ds(a * 256, 128), :] = own[:, 0:TOK]
        upper[pl.ds(a * 256 + 128, 128), :] = own[:, TOK:]

    def scatter(s):
        def one(j):
            to = dp_peer(j)
            pltpu.make_async_remote_copy(
                src_ref=small.at[s, to], dst_ref=rsmall.at[s, dp],
                send_sem=small_send.at[s], recv_sem=small_recv.at[s],
                device_id=(to, tn), device_id_type=MESH,
            ).start()

        tiles(NDP - 1, one)
        rsmall[s, dp] = small[s, dp]

    arrived(DM)

    def part_ld(d):
        v = dot(recv[DM, rows_at(d, 128), :], dy[...]).astype(BF)
        small[0, d, :, :] = v

    tiles(NDP, part_ld)
    scatter(0)
    out_o[...] = dot(ldt[...], recv[DM]).T.astype(BF)

    def part_in(s, i):
        def body(q):
            v = dot(xt[...], recv[i, rows_at(q, 256), :], NT).astype(BF)
            small[s, 2 * q, :, :] = jnp.concatenate([v[0:128, 0:128], v[128:256, 0:128]], axis=1)
            small[s, 2 * q + 1, :, :] = jnp.concatenate([v[0:128, 128:256], v[128:256, 128:256]], axis=1)

        tiles(4, body)
        scatter(s)

    arrived(DG)
    part_in(1, DG)
    dxt[...] = dot(rg[...], recv[DG])
    arrived(DU)
    part_in(2, DU)
    dx_o[...] = (dxt[...] + dot(ru[...], recv[DU])).T.astype(BF)

    for a, (_, _, out) in enumerate(big):
        started[a][4].wait_recv()
        out[0, :, 0:TOK] = (upper[pl.ds(a * 256, 128), :] + ye[a, :, 0:TOK].astype(F32)).astype(BF)
        out[0, :, TOK:] = (upper[pl.ds(a * 256 + 128, 128), :] + ye[a, :, TOK:].astype(F32)).astype(BF)

    def summed(s):
        await_bytes(rsmall.at[s, pl.ds(0, NDP - 1)], small_recv.at[s])
        v = rsmall[s, 0].astype(F32)
        for d in range(1, NDP):
            v = v + rsmall[s, d].astype(F32)
        return v.astype(BF)

    ld_o[0] = summed(0)
    for s, out in ((1, rg_o), (2, ru_o)):
        v = summed(s)
        out[0, 0:128, :] = v[:, 0:128]
        out[0, 128:256, :] = v[:, 128:256]

    for i in range(6):
        await_bytes(send.at[i, pl.ds(0, MB - KW)], a2a_send.at[i])
    for a in range(3):
        for cp in started[a]:
            cp.wait_send()
    for s in range(3):
        await_bytes(small.at[s, pl.ds(0, NDP - 1)], small_send.at[s])


def per_device(tokens, gate_in, gate_out, up_in, up_out, down_in, down_out, cotangent):
    anyw = pl.BlockSpec(memory_space=pl.ANY)
    vmem = pl.BlockSpec(memory_space=pltpu.VMEM)
    out_shape = (
        jax.ShapeDtypeStruct((TOK, DB), BF),
        jax.ShapeDtypeStruct((TOK, DB), BF),
        jax.ShapeDtypeStruct((1, DB, 128), BF),
        jax.ShapeDtypeStruct((1, 128, MB), BF),
        jax.ShapeDtypeStruct((1, DB, 128), BF),
        jax.ShapeDtypeStruct((1, 128, MB), BF),
        jax.ShapeDtypeStruct((1, 128, MB), BF),
        jax.ShapeDtypeStruct((1, 128, DB), BF),
    )
    V = pltpu.VMEM
    scratch = [
        V((TOK, DB), BF), V((DB, MB), BF), V((MB, MB), BF), V((DB, MB), BF), V((MB, MB), BF),
        V((MB, MB), BF), V((MB, DB), BF), V((TOK, DB), BF),
        V((DB, TOK), BF), V((MB, MB), BF), V((MB, MB), BF), V((MB, MB), BF), V((DB, MB), BF),
        V((6, MB, TOK), BF), V((6, MB, TOK), BF),
        V((MB, TOK), F32), V((MB, TOK), F32), V((MB, TOK), BF), V((MB, TOK), BF), V((MB, TOK), BF),
        V((DB, TOK), F32),
        V((3, 2, 128, MB), BF), V((3, 2, 128, MB), BF), V((3, 2, 128, MB), BF), V((3, 128, MB), BF),
        V((3, 128, MB), BF), V((3, 128, MB), BF), V((3, 2, 128, MB), BF), V((3, 2, 128, MB), BF), V((3, 128, MB), BF),
        V((3, NDP, 128, DB), BF), V((3, NDP, 128, DB), BF),
        pltpu.SemaphoreType.DMA((8,)), pltpu.SemaphoreType.DMA((6,)), pltpu.SemaphoreType.DMA((6,)),
        pltpu.SemaphoreType.DMA((15,)), pltpu.SemaphoreType.DMA((15,)),
        pltpu.SemaphoreType.DMA((3,)), pltpu.SemaphoreType.DMA((3,)),
    ]
    return pl.pallas_call(
        kernel,
        out_shape=out_shape,
        in_specs=[anyw] * 8,
        out_specs=(vmem,) * 8,
        scratch_shapes=scratch,
        compiler_params=pltpu.CompilerParams(
            collective_id=0, has_side_effects=True, vmem_limit_bytes=60 * 2**20
        ),
        cost_estimate=pl.CostEstimate(flops=12_000_000_000, bytes_accessed=10_000_000, transcendentals=1_000_000),
    )(tokens, gate_in, gate_out, up_in, up_out, down_in, down_out, cotangent)


def solution(mesh):
    in_specs = (
        P("dp", "tensor"),
        P("tensor", None, None),
        P("tensor", None, None),
        P("tensor", None, None),
        P("tensor", None, None),
        P("tensor", None, None),
        P("tensor", None, None),
        P("dp", "tensor"),
    )
    out_specs = (
        P("dp", "tensor"),
        P("dp", "tensor"),
        P("tensor", None, "dp"),
        P("tensor", "dp", None),
        P("tensor", None, "dp"),
        P("tensor", "dp", None),
        P("tensor", "dp", None),
        P("tensor", "dp", None),
    )
    return jax.shard_map(
        per_device, mesh=mesh, in_specs=in_specs, out_specs=out_specs, check_vma=False
    )
```

```python
import jax
import jax.numpy as jnp
from jax import lax
from jax.experimental import pallas as pl
from jax.experimental.pallas import tpu as pltpu
from jax.sharding import PartitionSpec as P

MESH = pl.DeviceIdType.MESH
BF = jnp.bfloat16
F32 = jnp.float32
NT = (((1,), (1,)), ((), ()))
NN = (((1,), (0,)), ((), ()))
TOK, HALF, DB, MB, KW, NBLK, NDP = 512, 256, 256, 1024, 32, 32, 8


def dot(a, b, form=NN):
    return lax.dot_general(a, b, form, preferred_element_type=F32)


def rows_at(index, size):
    return pl.ds(pl.multiple_of(index * size, size), size)


def tiles(count, body):
    def step(i, carry):
        body(i)
        return carry

    lax.fori_loop(0, count, step, 0)


def kernel(
    x_h, rg_h, lg_h, ru_h, lu_h, rd_h, ld_h, dy_h,
    out_o, dx_o, rg_o, lg_o, ru_o, lu_o, rd_o, ld_o,
    out_v, dx_v, rg_v, lg_v, ru_v, lu_v, rd_v, ld_v,
    xall, wt, wp, ps, rg, lg, ru, lu, rd, ld, dy,
    xt, lgt, lut, rdt, ldt,
    dsend, dd, rdd, send, recv, gum,
    gate, upper, hidden, dgate, dup, dxt,
    p2, pn, pp, ysend, ra, rb, rc, rdn, ye,
    small, rsmall,
    load_sem, store_sem, x_send, z_recv, c_recv, p_send, p_recv, d_send, d_recv, w_send, w_recv,
    a2a_send, a2a_recv, ring_send, ring_recv, small_send, small_recv,
):
    dp, tn = lax.axis_index("dp"), lax.axis_index("tensor")
    xc, yl = dp // 2, dp % 2
    yh, z, core = tn // 16, (tn // 2) % 8, tn % 2

    def block(y, zz, c):
        return (y * 8 + zz) * 2 + c

    def await_bytes(ref, sem):
        pltpu.make_async_copy(ref, ref, sem).wait()

    ring = z * 2 + core
    loads = {}
    for i, (name, src, dst) in enumerate((
        ("rg", rg_h.at[0], rg), ("ru", ru_h.at[0], ru),
        ("x0", x_h.at[pl.ds(0, HALF)], xall.at[0, ring]), ("x1", x_h.at[pl.ds(HALF, HALF)], xall.at[1, ring]),
        ("ld", ld_h.at[0], ld), ("dy", dy_h, dy), ("lg", lg_h.at[0], lg), ("lu", lu_h.at[0], lu), ("rd", rd_h.at[0], rd),
    )):
        loads[name] = pltpu.make_async_copy(src, dst, load_sem.at[i])
        loads[name].start()

    stores = []

    def store(src, dst):
        cp = pltpu.make_async_copy(src, dst, store_sem.at[len(stores)])
        cp.start()
        stores.append(cp)

    def peer(j):
        g = j // 4
        dz = 4 + (1 - 2 * (g % 2)) * ((g + 1) // 2)
        return block((yh + 1 - (j // 2) % 2) % 2, (z + dz) % 8, (core + 1 - j % 2) % 2)

    def dp_peer(j):
        return (dp + 1 + j) % NDP

    barrier = pltpu.get_barrier_semaphore()

    def greet_tensor(j):
        pl.semaphore_signal(barrier, inc=1, device_id=(dp, peer(j)), device_id_type=MESH)

    def greet_dp(j):
        pl.semaphore_signal(barrier, inc=1, device_id=(dp_peer(j), tn), device_id_type=MESH)

    tiles(NBLK - 1, greet_tensor)
    tiles(NDP - 1, greet_dp)

    OFFS = ((0, -1, 1, -2, 2, -3, 3, -4), (0, -1, 1, -2, 2, -3, 3, 4))

    def x_copy(h, b, sem, to):
        pltpu.make_async_remote_copy(
            src_ref=xall.at[h, b], dst_ref=xall.at[h, b], send_sem=x_send.at[h], recv_sem=sem,
            device_id=(dp, to), device_id_type=MESH,
        ).start()

    up_z, down_z = block(yh, (z + 1) % 8, core), block(yh, (z + 7) % 8, core)
    over_y, sibling = block(1 - yh, z, core), block(yh, z, 1 - core)

    def z_event(h, k):
        off = OFFS[h][k]
        b = ((z + off) % 8) * 2 + core
        if k:
            await_bytes(xall.at[h, b], z_recv.at[h, k])
        for sign, to in ((-1, up_z), (1, down_z)):
            if (off == 0 or off * sign > 0) and off + sign in OFFS[h]:
                x_copy(h, b, z_recv.at[h, OFFS[h].index(off + sign)], to)
        x_copy(h, b, c_recv.at[h, k], sibling)

    def flip(src, dst, across, r):
        def body(c):
            dst[rows_at(c, 256), pl.ds(r * 256, 256)] = src[pl.ds(r * 256, 256), rows_at(c, 256)].T

        tiles(across, body)

    def exchange(i, sem, *hs):
        mine = rows_at(tn, KW)

        def one(j):
            to = peer(j)
            pltpu.make_async_remote_copy(
                src_ref=send.at[(i, *hs, rows_at(to, KW))], dst_ref=recv.at[(i, *hs, mine)],
                send_sem=a2a_send.at[sem], recv_sem=a2a_recv.at[sem],
                device_id=(dp, to), device_id_type=MESH,
            ).start()

        tiles(NBLK - 1, one)
        recv[(i, *hs, mine)] = send[(i, *hs, mine)]

    BOTH = slice(None)

    def arrived(i, sem, h=BOTH):
        await_bytes(recv.at[i, h, pl.ds(0, MB - KW)], a2a_recv.at[sem])

    DM, DG, DU = range(3)

    loads["rg"].wait()
    loads["ru"].wait()

    @pl.when(xc < 2)
    def _():
        for r in range(4):
            wt[r // 2, pl.ds(r % 2 * 256, 256), :] = rg[:, pl.ds(r * 256, 256)].T

    @pl.when(xc >= 2)
    def _():
        for r in range(4):
            wt[r // 2, pl.ds(r % 2 * 256, 256), :] = ru[:, pl.ds(r * 256, 256)].T

    def w_rows(at):
        return pl.ds(pl.multiple_of(at * KW + (xc % 2) * 16, 16), 16)

    def send_w(j):
        at = (ring + 1 + j) % 16
        pltpu.make_async_remote_copy(
            src_ref=wt.at[:, w_rows(at)], dst_ref=wp.at[xc, ring], send_sem=w_send.at[0], recv_sem=w_recv.at[0],
            device_id=(dp, yh * 16 + at), device_id_type=MESH,
        ).start()

    pl.semaphore_wait(barrier, NBLK - 1 + NDP - 1)
    tiles(15, send_w)
    loads["x0"].wait()
    z_event(0, 0)
    loads["x1"].wait()
    z_event(1, 0)
    wp[xc, ring] = wt[:, w_rows(ring), :]

    loads["dy"].wait()
    loads["ld"].wait()

    def back_down(q):
        rows = rows_at(q, 256)
        for h in range(2):
            toks = dy[h * HALF:(h + 1) * HALF, :]
            dsend[h, rows, :] = dot(ld[pl.ds(pl.multiple_of((1 - yh) * 512 + q * 256, 256), 256), :], toks, NT).astype(BF)
            dd[yh, h, rows, :] = dot(ld[pl.ds(pl.multiple_of(yh * 512 + q * 256, 256), 256), :], toks, NT).astype(BF)

    tiles(2, back_down)
    to_y = pltpu.make_async_remote_copy(
        src_ref=dsend, dst_ref=dd.at[yh], send_sem=d_send.at[0], recv_sem=d_recv.at[0],
        device_id=(dp, over_y), device_id_type=MESH,
    )
    to_y.start()

    def relay():
        to_y.wait_recv()

        def one(j):
            at = (ring + 1 + j) % 16
            pltpu.make_async_remote_copy(
                src_ref=dd.at[:, :, rows_at(at, KW)], dst_ref=rdd.at[:, :, rows_at(ring, KW)],
                send_sem=d_send.at[1], recv_sem=d_recv.at[1], device_id=(dp, yh * 16 + at), device_id_type=MESH,
            ).start()

        tiles(15, one)
        rdd[:, :, rows_at(ring, KW), :] = dd[:, :, rows_at(ring, KW), :]

    loads["lg"].wait()
    for r in range(4):
        flip(lg, lgt, 4, r)

    await_bytes(wp.at[0, pl.ds(0, 15)], w_recv.at[0])

    def share_w(j):
        to = ((xc + 1 + j) % 4) * 2 + yl
        pltpu.make_async_remote_copy(
            src_ref=wp.at[xc], dst_ref=wp.at[xc], send_sem=w_send.at[1], recv_sem=w_recv.at[1],
            device_id=(to, tn), device_id_type=MESH,
        ).start()

    tiles(3, share_w)

    def first(h, *ks):
        for k in ks:
            await_bytes(xall.at[h, 0], c_recv.at[h, k])
            at = (z + OFFS[h][k]) % 8

            def body(c, at=at):
                b = at * 2 + c
                w = jnp.concatenate([wp[p, b, y] for y in (yh, 1 - yh) for p in range(4)], axis=0)
                v = dot(w, xall[h, b], NT).astype(BF)
                own, rows = rows_at(yh * 16 + b, KW), rows_at(b, KW)
                gum[h, 0, own, :] = v[0:32]
                gum[h, 1, own, :] = v[32:64]
                ps[h, 0, rows, :] = v[64:96]
                ps[h, 1, rows, :] = v[96:128]
                pltpu.make_async_remote_copy(
                    src_ref=ps.at[h, :, rows], dst_ref=gum.at[h, :, own], send_sem=p_send.at[h], recv_sem=p_recv.at[h],
                    device_id=(dp, over_y), device_id_type=MESH,
                ).start()

            tiles(2, body)

    def events(h, *ks):
        for k in ks:
            z_event(h, k)

    loads["lu"].wait()
    for r in range(4):
        flip(lu, lut, 4, r)
    events(0, 1, 2)
    events(1, 1, 2)
    loads["rd"].wait()
    for r in range(4):
        flip(rd, rdt, 4, r)
    events(0, 3, 4)
    events(1, 3, 4)
    for h in range(2):
        xt[h] = xall[h, ring].T
    for r in range(4):
        flip(ld, ldt, 1, r)
    await_bytes(wp.at[pl.ds(0, 3)], w_recv.at[1])
    first(0, 0, 1, 2, 3, 4)
    events(0, 5, 6)
    events(1, 5, 6)
    first(0, 5, 6)
    first(1, 0, 1, 2)
    events(0, 7)
    events(1, 7)
    relay()
    first(0, 7)
    first(1, 3, 4, 5, 6, 7)

    def forward(h):
        await_bytes(gum.at[h, :, pl.ds(0, 512)], p_recv.at[h])

        def body(q):
            rows = rows_at(q, 256)
            g = dot(lgt[rows, :], gum[h, 0])
            u = dot(lut[rows, :], gum[h, 1])
            gate[h, rows, :] = g
            upper[h, rows, :] = u
            hidden[h, rows, :] = (g * jax.nn.sigmoid(g) * u).astype(BF)

        tiles(4, body)

        def down(q):
            rows = rows_at(q, 256)
            send[DM, h, rows, :] = dot(rdt[rows, :], hidden[h]).astype(BF)

        tiles(4, down)
        exchange(DM, h, h)

    forward(0)
    forward(1)
    await_bytes(rdd.at[:, :, pl.ds(0, 480)], d_recv.at[1])

    def backward(h):
        def body(q):
            rows = rows_at(q, 256)
            dh = dot(rd[rows, 0:512], rdd[0, h]) + dot(rd[rows, 512:1024], rdd[1, h])
            g, u = gate[h, rows, :], upper[h, rows, :]
            s = jax.nn.sigmoid(g)
            dgate[h, rows, :] = (dh * u * s * (1.0 + g * (1.0 - s))).astype(BF)
            dup[h, rows, :] = (dh * (g * s)).astype(BF)

        tiles(4, body)

    def mids(i, sem, w, d):
        def body(q):
            rows = rows_at(q, 256)
            for h in range(2):
                send[i, h, rows, :] = dot(w[rows, :], d[h]).astype(BF)

        tiles(4, body)
        exchange(i, sem, BOTH)

    backward(0)
    backward(1)
    mids(DG, 2, lg, dgate)
    mids(DU, 3, lu, dup)

    nxt, prv, opp = (xc + 1) % 4, (xc + 3) % 4, (xc + 2) % 4

    def ship(src, dst, sem, to):
        cp = pltpu.make_async_remote_copy(
            src_ref=src, dst_ref=dst, send_sem=ring_send.at[sem], recv_sem=ring_recv.at[sem],
            device_id=to, device_id_type=MESH,
        )
        cp.start()
        return cp

    to_next, to_prev = (nxt * 2 + yl, tn), (prv * 2 + yl, tn)
    to_pair = (xc * 2 + 1 - yl, tn)
    big = (
        (hidden, rdd, rd_v, rd_o),
        (gum.at[:, 0], dgate, lg_v, lg_o),
        (gum.at[:, 1], dup, lu_v, lu_o),
    )

    def part(left, right, q, half):
        rows = pl.ds(pl.multiple_of(q * 256 + half * 128, 128), 128)

        def both(pick):
            return dot(left[0, rows, :], pick(0), NT) + dot(left[1, rows, :], pick(1), NT)

        if right is rdd:
            return jnp.concatenate([both(lambda h, y=y: rdd[y, h]) for y in range(2)], axis=1)
        return both(lambda h: right[h])

    def quarter(left, right, q, put):
        tiles(2, lambda half: put(half, part(left, right, q, half)))

    started = [[None] * 5 for _ in big]
    for a, (left, right, _, _) in enumerate(big):
        def put(half, v, a=a):
            p2[a, half] = v.astype(BF)

        quarter(left, right, opp, put)
        started[a][0] = ship(p2.at[a, 0], ra.at[a], 5 * a, to_next)
        started[a][1] = ship(p2.at[a, 1], rb.at[a], 5 * a + 1, to_prev)
    for a, (left, right, _, _) in enumerate(big):
        def put_n(half, v, a=a):
            pn[a, half] = v.astype(BF)

        def put_p(half, v, a=a):
            pp[a, half] = v.astype(BF)

        quarter(left, right, nxt, put_n)
        started[a][0].wait_recv()
        pn[a, 0] = (pn[a, 0].astype(F32) + ra[a].astype(F32)).astype(BF)
        started[a][2] = ship(pn.at[a], rc.at[a], 5 * a + 2, to_next)
        quarter(left, right, prv, put_p)
        started[a][1].wait_recv()
        pp[a, 1] = (pp[a, 1].astype(F32) + rb[a].astype(F32)).astype(BF)
        started[a][3] = ship(pp.at[a], rdn.at[a], 5 * a + 3, to_prev)

    def kept(a, c):
        return c % 2, pl.ds((a * 2 + c // 2) * 128, 128)

    for a, (left, right, _, _) in enumerate(big):
        started[a][2].wait_recv()
        started[a][3].wait_recv()

        def total(half, a=a, left=left, right=right):
            return part(left, right, xc, half) + rc[a, half].astype(F32) + rdn[a, half].astype(F32)

        ysend[a] = total(1 - yl).astype(BF)
        started[a][4] = ship(ysend.at[a], ye.at[a], 5 * a + 4, to_pair)
        own = total(yl)
        for c in range(4):
            s, rows = kept(a, c)
            upper[s, rows, :] = own[:, c * 256:(c + 1) * 256]

    def scatter(s):
        def one(j):
            to = dp_peer(j)
            pltpu.make_async_remote_copy(
                src_ref=small.at[s, to], dst_ref=rsmall.at[s, dp],
                send_sem=small_send.at[s], recv_sem=small_recv.at[s],
                device_id=(to, tn), device_id_type=MESH,
            ).start()

        tiles(NDP - 1, one)
        rsmall[s, dp] = small[s, dp]

    arrived(DM, 0, 0)
    arrived(DM, 1, 1)

    def part_ld(d):
        rows = rows_at(d, 128)
        v = dot(recv[DM, 0, rows, :], dy[0:HALF, :]) + dot(recv[DM, 1, rows, :], dy[HALF:, :])
        small[0, d, :, :] = v.astype(BF)

    tiles(NDP, part_ld)
    scatter(0)
    for h in range(2):
        out_v[h * HALF:(h + 1) * HALF, :] = dot(ldt[...], recv[DM, h]).T.astype(BF)
    store(out_v, out_o)

    def part_in(s, i):
        def body(q):
            rows = rows_at(q, 256)
            v = (dot(xt[0], recv[i, 0, rows, :], NT) + dot(xt[1], recv[i, 1, rows, :], NT)).astype(BF)
            small[s, 2 * q, :, :] = jnp.concatenate([v[0:128, 0:128], v[128:256, 0:128]], axis=1)
            small[s, 2 * q + 1, :, :] = jnp.concatenate([v[0:128, 128:256], v[128:256, 128:256]], axis=1)

        tiles(4, body)
        scatter(s)

    arrived(DG, 2)
    part_in(1, DG)
    for h in range(2):
        dxt[h] = dot(rg[...], recv[DG, h])
    for a, (_, _, out, out_h) in enumerate(big):
        started[a][4].wait_recv()
        for c in range(4):
            s, rows = kept(a, c)
            cols = slice(c * 256, (c + 1) * 256)
            out[:, cols] = (upper[s, rows, :] + ye[a, :, cols].astype(F32)).astype(BF)
        store(out, out_h.at[0])

    arrived(DU, 3)
    part_in(2, DU)
    for h in range(2):
        dx_v[h * HALF:(h + 1) * HALF, :] = (dxt[h] + dot(ru[...], recv[DU, h])).T.astype(BF)
    store(dx_v, dx_o)

    def summed(s):
        await_bytes(rsmall.at[s, pl.ds(0, NDP - 1)], small_recv.at[s])
        v = rsmall[s, 0].astype(F32)
        for d in range(1, NDP):
            v = v + rsmall[s, d].astype(F32)
        return v.astype(BF)

    ld_v[...] = summed(0)
    store(ld_v, ld_o.at[0])
    for s, out, out_h in ((1, rg_v, rg_o), (2, ru_v, ru_o)):
        v = summed(s)
        out[0:128, :] = v[:, 0:128]
        out[128:256, :] = v[:, 128:256]
        store(out, out_h.at[0])

    for h in range(2):
        await_bytes(xall.at[h, pl.ds(0, 15)], x_send.at[h])
        await_bytes(ps.at[h], p_send.at[h])
        await_bytes(send.at[DM, h, pl.ds(0, MB - KW)], a2a_send.at[h])
    to_y.wait_send()
    await_bytes(rdd.at[:, :, pl.ds(0, 480)], d_send.at[1])
    for i, sem in ((DG, 2), (DU, 3)):
        await_bytes(send.at[i, :, pl.ds(0, MB - KW)], a2a_send.at[sem])
    await_bytes(wp.at[0, pl.ds(0, 15)], w_send.at[0])
    await_bytes(wp.at[pl.ds(0, 3)], w_send.at[1])
    for a in range(3):
        for cp in started[a]:
            cp.wait_send()
    for s in range(3):
        await_bytes(small.at[s, pl.ds(0, NDP - 1)], small_send.at[s])
    for cp in stores:
        cp.wait()


def hand_over(*refs):
    src, dst, held, (sem,) = refs[:8], refs[8:16], refs[16:24], refs[24:]
    arriving = [pltpu.make_async_copy(src[i], held[i], sem.at[0, i]) for i in range(8)]
    leaving = [pltpu.make_async_copy(held[i], dst[i], sem.at[1, i]) for i in range(8)]
    for cp in arriving:
        cp.start()
    for i in range(8):
        arriving[i].wait()
        leaving[i].start()
    for cp in leaving:
        cp.wait()


def per_device(tokens, gate_in, gate_out, up_in, up_out, down_in, down_out, cotangent):
    anyw = pl.BlockSpec(memory_space=pl.ANY)
    out_shape = (
        jax.ShapeDtypeStruct((TOK, DB), BF),
        jax.ShapeDtypeStruct((TOK, DB), BF),
        jax.ShapeDtypeStruct((1, DB, 128), BF),
        jax.ShapeDtypeStruct((1, 128, MB), BF),
        jax.ShapeDtypeStruct((1, DB, 128), BF),
        jax.ShapeDtypeStruct((1, 128, MB), BF),
        jax.ShapeDtypeStruct((1, 128, MB), BF),
        jax.ShapeDtypeStruct((1, 128, DB), BF),
    )
    V = pltpu.VMEM
    mids = V((2, MB, HALF), BF)
    wide = V((2, MB, HALF), F32)
    square = V((MB, MB), BF)
    dma = pltpu.SemaphoreType.DMA
    scratch = [
        V((TOK, DB), BF), V((TOK, DB), BF), V((DB, 128), BF), V((128, MB), BF),
        V((DB, 128), BF), V((128, MB), BF), V((128, MB), BF), V((128, DB), BF),
        V((2, 16, HALF, DB), BF), V((2, 512, DB), BF), V((4, 16, 2, 16, DB), BF), V((2, 2, 512, HALF), BF),
        V((DB, MB), BF), square, V((DB, MB), BF), square, square, V((MB, DB), BF), V((TOK, DB), BF),
        V((2, DB, HALF), BF), square, square, square, V((DB, MB), BF),
        V((2, 512, HALF), BF), V((2, 2, 512, HALF), BF), V((2, 2, 512, HALF), BF),
        V((3, 2, MB, HALF), BF), V((3, 2, MB, HALF), BF), V((2, 2, MB, HALF), BF),
        wide, wide, mids, mids, mids, V((2, DB, HALF), F32),
        V((3, 2, 128, MB), BF), V((3, 2, 128, MB), BF), V((3, 2, 128, MB), BF), V((3, 128, MB), BF),
        V((3, 128, MB), BF), V((3, 128, MB), BF), V((3, 2, 128, MB), BF), V((3, 2, 128, MB), BF), V((3, 128, MB), BF),
        V((3, NDP, 128, DB), BF), V((3, NDP, 128, DB), BF),
        dma((9,)), dma((8,)), dma((2,)), dma((2, 8)), dma((2, 8)), dma((2,)), dma((2,)), dma((2,)), dma((2,)), dma((2,)), dma((2,)),
        dma((4,)), dma((4,)), dma((15,)), dma((15,)), dma((3,)), dma((3,)),
    ]
    results = pl.pallas_call(
        kernel,
        out_shape=out_shape,
        in_specs=[anyw] * 8,
        out_specs=(anyw,) * 8,
        scratch_shapes=scratch,
        compiler_params=pltpu.CompilerParams(
            collective_id=0, has_side_effects=True, vmem_limit_bytes=62 * 2**20
        ),
        cost_estimate=pl.CostEstimate(flops=12_000_000_000, bytes_accessed=10_000_000, transcendentals=1_000_000),
    )(tokens, gate_in, gate_out, up_in, up_out, down_in, down_out, cotangent)
    return pl.pallas_call(
        hand_over,
        out_shape=out_shape,
        in_specs=[anyw] * 8,
        out_specs=(anyw,) * 8,
        scratch_shapes=[V(o.shape, BF) for o in out_shape] + [pltpu.SemaphoreType.DMA((2, 8))],
    )(*results)


def solution(mesh):
    in_specs = (
        P("dp", "tensor"),
        P("tensor", None, None),
        P("tensor", None, None),
        P("tensor", None, None),
        P("tensor", None, None),
        P("tensor", None, None),
        P("tensor", None, None),
        P("dp", "tensor"),
    )
    out_specs = (
        P("dp", "tensor"),
        P("dp", "tensor"),
        P("tensor", None, "dp"),
        P("tensor", "dp", None),
        P("tensor", None, "dp"),
        P("tensor", "dp", None),
        P("tensor", "dp", None),
        P("tensor", "dp", None),
    )
    return jax.shard_map(
        per_device, mesh=mesh, in_specs=in_specs, out_specs=out_specs, check_vma=False
    )
```

```python
import jax
import jax.numpy as jnp
from jax import lax
from jax.experimental import pallas as pl
from jax.experimental.pallas import tpu as pltpu
from jax.sharding import PartitionSpec as P

MESH = pl.DeviceIdType.MESH
BF = jnp.bfloat16
F32 = jnp.float32
NT = (((1,), (1,)), ((), ()))
NN = (((1,), (0,)), ((), ()))
TN = (((0,), (0,)), ((), ()))
TOK, HALF, DB, MB, KW, NBLK, NDP = 512, 256, 256, 1024, 32, 32, 8


def dot(a, b, form=NN):
    return lax.dot_general(a, b, form, preferred_element_type=F32)


def rows_at(index, size):
    return pl.ds(pl.multiple_of(index * size, size), size)


def tiles(count, body):
    def step(i, carry):
        body(i)
        return carry

    lax.fori_loop(0, count, step, 0)


def kernel(
    x_h, rg_h, lg_h, ru_h, lu_h, rd_h, ld_h, dy_h,
    out_o, dx_o, rg_o, lg_o, ru_o, lu_o, rd_o, ld_o,
    out_v, dx_v, rg_v, lg_v, ru_v, lu_v, rd_v, ld_v,
    xall, wt, wp, ps, rg, lg, ru, lu, rd, ld, dy,
    lgt, lut, rdt, ldt,
    dsend, dd, rdd, msend, dm, rdm, gum, back, sums_in, chain_in,
    gate, upper, hidden, dgate, dup,
    p2, pn, pp, ysend, ra, rb, rc, rdn, ye,
    wring, lring, wown, lown, wsum, wfin,
    load_sem, store_sem, x_send, z_recv, c_recv, p_send, p_recv, d_send, d_recv, w_send, w_recv,
    m_send, m_recv, ring_send, ring_recv,
    b_send, b_recv, s_send, s_recv, ch_send, ch_recv, wf_send, wf_recv,
):
    dp, tn = lax.axis_index("dp"), lax.axis_index("tensor")
    xc, yl = dp // 2, dp % 2
    yh, z, core = tn // 16, (tn // 2) % 8, tn % 2

    def block(y, zz, c):
        return (y * 8 + zz) * 2 + c

    def await_bytes(ref, sem):
        pltpu.make_async_copy(ref, ref, sem).wait()

    ring = z * 2 + core
    loads = {}
    for i, (name, src, dst) in enumerate((
        ("rg", rg_h.at[0], rg), ("ru", ru_h.at[0], ru),
        ("x0", x_h.at[pl.ds(0, HALF)], xall.at[0, ring]), ("x1", x_h.at[pl.ds(HALF, HALF)], xall.at[1, ring]),
        ("ld", ld_h.at[0], ld), ("dy", dy_h, dy), ("lg", lg_h.at[0], lg), ("lu", lu_h.at[0], lu), ("rd", rd_h.at[0], rd),
    )):
        loads[name] = pltpu.make_async_copy(src, dst, load_sem.at[i])
        loads[name].start()

    stores = []

    def store(src, dst):
        cp = pltpu.make_async_copy(src, dst, store_sem.at[len(stores)])
        cp.start()
        stores.append(cp)

    def peer(j):
        g = j // 4
        dz = 4 + (1 - 2 * (g % 2)) * ((g + 1) // 2)
        return block((yh + 1 - (j // 2) % 2) % 2, (z + dz) % 8, (core + 1 - j % 2) % 2)

    def dp_peer(j):
        return (dp + 2 * j + 2) % NDP

    barrier = pltpu.get_barrier_semaphore()

    def greet_tensor(j):
        pl.semaphore_signal(barrier, inc=1, device_id=(dp, peer(j)), device_id_type=MESH)

    def greet_dp(j):
        pl.semaphore_signal(barrier, inc=1, device_id=(dp_peer(j), tn), device_id_type=MESH)

    tiles(NBLK - 1, greet_tensor)
    tiles(3, greet_dp)
    pl.semaphore_signal(barrier, inc=1, device_id=(xc * 2 + 1 - yl, tn), device_id_type=MESH)

    def apart(to_dp, to_tn, here, there):
        same = jnp.logical_and(to_dp == dp, to_tn == tn)
        pl.when(same)(here)
        pl.when(jnp.logical_not(same))(there)

    def summed_block(d, par):
        return ((z + (d if par == 0 else 8 - d)) % 8) * 2 + par

    for j in range(4):
        away = 8 + z - (2 * (dp % 4) + j // 2)
        source = ((away * (1 + 6 * core)) % 8, yh * 16 + 4 * (dp % 4) + j)

        def greet_source(source=source):
            pl.semaphore_signal(barrier, inc=1, device_id=source, device_id_type=MESH)

        apart(*source, lambda: None, greet_source)
    stays = jnp.logical_and(dp == 0, z < 2).astype(jnp.int32)

    OFFS = ((0, -1, 1, -2, 2, -3, 3, -4), (0, -1, 1, -2, 2, -3, 3, 4))

    def x_copy(h, b, sem, to):
        pltpu.make_async_remote_copy(
            src_ref=xall.at[h, b], dst_ref=xall.at[h, b], send_sem=x_send.at[h], recv_sem=sem,
            device_id=(dp, to), device_id_type=MESH,
        ).start()

    up_z, down_z = block(yh, (z + 1) % 8, core), block(yh, (z + 7) % 8, core)
    over_y, sibling = block(1 - yh, z, core), block(yh, z, 1 - core)

    def z_event(h, k):
        off = OFFS[h][k]
        b = ((z + off) % 8) * 2 + core
        if k:
            await_bytes(xall.at[h, b], z_recv.at[h, k])
        for sign, to in ((-1, up_z), (1, down_z)):
            if (off == 0 or off * sign > 0) and off + sign in OFFS[h]:
                x_copy(h, b, z_recv.at[h, OFFS[h].index(off + sign)], to)
        x_copy(h, b, c_recv.at[h, k], sibling)

    def flip(src, dst, across, r):
        def body(c):
            dst[rows_at(c, 256), pl.ds(r * 256, 256)] = src[pl.ds(r * 256, 256), rows_at(c, 256)].T

        tiles(across, body)

    loads["rg"].wait()
    loads["ru"].wait()

    @pl.when(xc < 2)
    def _():
        for r in range(4):
            wt[r // 2, pl.ds(r % 2 * 256, 256), :] = rg[:, pl.ds(r * 256, 256)].T

    @pl.when(xc >= 2)
    def _():
        for r in range(4):
            wt[r // 2, pl.ds(r % 2 * 256, 256), :] = ru[:, pl.ds(r * 256, 256)].T

    def w_rows(at):
        return pl.ds(pl.multiple_of(at * KW + (xc % 2) * 16, 16), 16)

    def send_w(j):
        at = (ring + 1 + j) % 16
        pltpu.make_async_remote_copy(
            src_ref=wt.at[:, w_rows(at)], dst_ref=wp.at[xc, ring], send_sem=w_send.at[0], recv_sem=w_recv.at[0],
            device_id=(dp, yh * 16 + at), device_id_type=MESH,
        ).start()

    pl.semaphore_wait(barrier, NBLK - 1 + 3 + 1 + 4 - stays)
    tiles(15, send_w)
    loads["x0"].wait()
    z_event(0, 0)
    loads["x1"].wait()
    z_event(1, 0)
    wp[xc, ring] = wt[:, w_rows(ring), :]

    loads["dy"].wait()
    loads["ld"].wait()

    def back_down(q):
        rows = rows_at(q, 256)
        for h in range(2):
            toks = dy[h * HALF:(h + 1) * HALF, :]
            dsend[h, rows, :] = dot(ld[pl.ds(pl.multiple_of((1 - yh) * 512 + q * 256, 256), 256), :], toks, NT).astype(BF)
            dd[yh, h, rows, :] = dot(ld[pl.ds(pl.multiple_of(yh * 512 + q * 256, 256), 256), :], toks, NT).astype(BF)

    tiles(2, back_down)
    to_y = pltpu.make_async_remote_copy(
        src_ref=dsend, dst_ref=dd.at[yh], send_sem=d_send.at[0], recv_sem=d_recv.at[0],
        device_id=(dp, over_y), device_id_type=MESH,
    )
    to_y.start()

    def relay(held, dst, send_sem, recv_sem):
        def one(j):
            at = (ring + 1 + j) % 16
            pltpu.make_async_remote_copy(
                src_ref=held.at[:, :, rows_at(at, KW)], dst_ref=dst.at[:, :, rows_at(ring, KW)],
                send_sem=send_sem, recv_sem=recv_sem, device_id=(dp, yh * 16 + at), device_id_type=MESH,
            ).start()

        tiles(15, one)
        dst[:, :, rows_at(ring, KW), :] = held[:, :, rows_at(ring, KW), :]

    def flip_blocks(src, dst):
        def body(i):
            r, c = i // 4, i % 4
            dst[c * 4 + r] = src[rows_at(r, 256), rows_at(c, 256)].T

        tiles(16, body)

    def block_row(t, q):
        return jnp.concatenate([t[q * 4 + c] for c in range(4)], axis=1)

    loads["lg"].wait()
    flip_blocks(lg, lgt)

    await_bytes(wp.at[0, pl.ds(0, 15)], w_recv.at[0])

    def share_w(j):
        to = ((xc + 1 + j) % 4) * 2 + yl
        pltpu.make_async_remote_copy(
            src_ref=wp.at[xc], dst_ref=wp.at[xc], send_sem=w_send.at[1], recv_sem=w_recv.at[1],
            device_id=(to, tn), device_id_type=MESH,
        ).start()

    tiles(3, share_w)

    def columns(b, *ys):
        return jnp.concatenate([wp[p, b, y] for y in ys for p in range(4)], axis=0)

    def first(h, *ks):
        for k in ks:
            await_bytes(xall.at[h, 0], c_recv.at[h, k])
            at = (z + OFFS[h][k]) % 8

            def body(c, at=at):
                b = at * 2 + c
                w = columns(b, yh, 1 - yh)
                v = dot(w, xall[h, b], NT).astype(BF)
                own, rows = rows_at(yh * 16 + b, KW), rows_at(b, KW)
                gum[h, 0, own, :] = v[0:32]
                gum[h, 1, own, :] = v[32:64]
                ps[h, 0, rows, :] = v[64:96]
                ps[h, 1, rows, :] = v[96:128]
                pltpu.make_async_remote_copy(
                    src_ref=ps.at[h, :, rows], dst_ref=gum.at[h, :, own], send_sem=p_send.at[h], recv_sem=p_recv.at[h],
                    device_id=(dp, over_y), device_id_type=MESH,
                ).start()

            tiles(2, body)

    def events(h, *ks):
        for k in ks:
            z_event(h, k)

    loads["lu"].wait()
    flip_blocks(lu, lut)
    events(0, 1, 2)
    events(1, 1, 2)
    loads["rd"].wait()
    for r in range(4):
        flip(rd, rdt, 4, r)
    events(0, 3, 4)
    events(1, 3, 4)
    for r in range(4):
        flip(ld, ldt, 1, r)
    await_bytes(wp.at[pl.ds(0, 3)], w_recv.at[1])
    first(0, 0, 1, 2, 3, 4)
    events(0, 5, 6)
    events(1, 5, 6)
    first(0, 5, 6)
    first(1, 0, 1, 2)
    events(0, 7)
    events(1, 7)
    to_y.wait_recv()
    relay(dd, rdd, d_send.at[1], d_recv.at[1])
    first(0, 7)
    first(1, 3, 4, 5, 6, 7)

    downs = []

    def forward(h):
        await_bytes(gum.at[h, :, pl.ds(0, 512)], p_recv.at[h])

        def body(q):
            rows = rows_at(q, 256)
            g = dot(block_row(lgt, q), gum[h, 0])
            u = dot(block_row(lut, q), gum[h, 1])
            gate[h, rows, :] = g
            upper[h, rows, :] = u
            hidden[h, rows, :] = (g * jax.nn.sigmoid(g) * u).astype(BF)

        tiles(4, body)

        def down_over(q):
            rows = pl.ds(pl.multiple_of((1 - yh) * 512 + q * 256, 256), 256)
            msend[h, rows_at(q, 256), :] = dot(rdt[rows, :], hidden[h]).astype(BF)

        tiles(2, down_over)
        cp = pltpu.make_async_remote_copy(
            src_ref=msend.at[h], dst_ref=dm.at[yh, h], send_sem=m_send.at[h], recv_sem=m_recv.at[h],
            device_id=(dp, over_y), device_id_type=MESH,
        )
        cp.start()
        downs.append(cp)

        def down_here(q):
            rows = pl.ds(pl.multiple_of(yh * 512 + q * 256, 256), 256)
            dm[yh, h, rows_at(q, 256), :] = dot(rdt[rows, :], hidden[h]).astype(BF)

        tiles(2, down_here)

    forward(0)
    forward(1)
    await_bytes(rdd.at[:, :, pl.ds(0, 480)], d_recv.at[1])

    def backward(h):
        def body(q):
            rows = rows_at(q, 256)
            dh = dot(rd[rows, 0:512], rdd[0, h]) + dot(rd[rows, 512:1024], rdd[1, h])
            g, u = gate[h, rows, :], upper[h, rows, :]
            s = jax.nn.sigmoid(g)
            dgate[h, rows, :] = (dh * u * s * (1.0 + g * (1.0 - s))).astype(BF)
            dup[h, rows, :] = (dh * (g * s)).astype(BF)

        tiles(4, body)

    nxt, prv, opp = (xc + 1) % 4, (xc + 3) % 4, (xc + 2) % 4

    def ship(src, dst, sem, to):
        cp = pltpu.make_async_remote_copy(
            src_ref=src, dst_ref=dst, send_sem=ring_send.at[sem], recv_sem=ring_recv.at[sem],
            device_id=to, device_id_type=MESH,
        )
        cp.start()
        return cp

    to_next, to_prev = (nxt * 2 + yl, tn), (prv * 2 + yl, tn)
    to_pair = (xc * 2 + 1 - yl, tn)
    big = (
        (hidden, rdd, rd_v, rd_o),
        (gum.at[:, 0], dgate, lg_v, lg_o),
        (gum.at[:, 1], dup, lu_v, lu_o),
    )

    def part(a, q, half):
        if a == 3:
            return jnp.concatenate([part_in(summed_block(2 * q + half, par)) for par in range(2)], axis=0)
        rows = pl.ds(pl.multiple_of(q * 256 + half * 128, 128), 128)
        if a == 4:
            inner = pl.ds(pl.multiple_of(q % 2 * 256 + half * 128, 128), 128)
            return dot(rdm[q // 2, 0, inner, :], dy[0:HALF, :]) + dot(rdm[q // 2, 1, inner, :], dy[HALF:, :])
        left, right = big[a][:2]

        def both(pick):
            return dot(left[0, rows, :], pick(0), NT) + dot(left[1, rows, :], pick(1), NT)

        if a == 0:
            return jnp.concatenate([both(lambda h, y=y: rdd[y, h]) for y in range(2)], axis=1)
        return both(lambda h: right[h])

    started = [[None] * 5 for _ in range(5)]
    places = [tuple(ref.at[a] for ref in (p2, pn, pp, ysend, ra, rb, rc, rdn, ye)) for a in range(3)]
    for ref in (wring, lring):
        places.append(tuple(
            ref.at[at] if size == 1 else ref.at[pl.ds(at, size)]
            for at, size in ((0, 2), (2, 2), (4, 2), (6, 1), (7, 1), (8, 1), (9, 2), (11, 2), (13, 1))
        ))

    def ring1(a):
        p2, _, _, _, ra, rb = places[a][:6]

        def put(half):
            p2[half] = part(a, opp, half).astype(BF)

        tiles(2, put)
        started[a][0] = ship(p2.at[0], ra, 5 * a, to_next)
        started[a][1] = ship(p2.at[1], rb, 5 * a + 1, to_prev)

    def ring2(a):
        _, pn, pp, _, ra, rb, rc, rdn, _ = places[a]

        def put_n(half):
            pn[half] = part(a, nxt, half).astype(BF)

        def put_p(half):
            pp[half] = part(a, prv, half).astype(BF)

        tiles(2, put_n)
        started[a][0].wait_recv()
        pn[0] = (pn[0].astype(F32) + ra[...].astype(F32)).astype(BF)
        started[a][2] = ship(pn, rc, 5 * a + 2, to_next)
        tiles(2, put_p)
        started[a][1].wait_recv()
        pp[1] = (pp[1].astype(F32) + rb[...].astype(F32)).astype(BF)
        started[a][3] = ship(pp, rdn, 5 * a + 3, to_prev)

    def kept(a, c):
        return c % 2, pl.ds((a * 2 + c // 2) * 128, 128)

    def ring3(a):
        _, _, _, ysend, _, _, rc, rdn, ye = places[a]
        started[a][2].wait_recv()
        started[a][3].wait_recv()

        def total(half):
            return part(a, xc, half) + rc[half].astype(F32) + rdn[half].astype(F32)

        ysend[...] = total(1 - yl).astype(BF)
        started[a][4] = ship(ysend, ye, 5 * a + 4, to_pair)
        own = total(yl)
        if a >= 3:
            (wown, lown)[a - 3][...] = own
            return
        for c in range(4):
            s, rows = kept(a, c)
            upper[s, rows, :] = own[:, c * 256:(c + 1) * 256]

    def ring4(a):
        ye = places[a][8]
        started[a][4].wait_recv()
        if a == 3:
            wsum[...] = (wown[...] + ye[...].astype(F32)).astype(BF)
            return
        if a == 4:
            ld_v[...] = (lown[...] + ye[...].astype(F32)).astype(BF)
            store(ld_v, ld_o.at[0])
            return
        out, out_h = big[a][2:]
        for c in range(4):
            s, rows = kept(a, c)
            cols = slice(c * 256, (c + 1) * 256)
            out[:, cols] = (upper[s, rows, :] + ye[:, cols].astype(F32)).astype(BF)
        store(out, out_h.at[0])

    for h in range(2):
        await_bytes(ps.at[h], p_send.at[h])
    crossing = []

    def mids_over(gu, w, d):
        def body(q):
            src = pl.ds(pl.multiple_of((1 - yh) * 512 + q * 256, 256), 256)
            for h in range(2):
                ps[gu, h, rows_at(q, 256), :] = dot(w[src, :], d[h]).astype(BF)

        tiles(2, body)
        cp = pltpu.make_async_remote_copy(
            src_ref=ps.at[gu], dst_ref=back.at[yh, gu], send_sem=b_send.at[gu], recv_sem=b_recv.at[gu],
            device_id=(dp, over_y), device_id_type=MESH,
        )
        cp.start()
        crossing.append(cp)

    def mids_here(gu, w, d):
        def body(q):
            src = pl.ds(pl.multiple_of(yh * 512 + q * 256, 256), 256)
            for h in range(2):
                back[yh, gu, h, rows_at(q, 256), :] = dot(w[src, :], d[h]).astype(BF)

        tiles(2, body)

    ring1(0)
    backward(0)
    backward(1)
    mids_over(0, lg, dgate)
    ring1(1)
    mids_over(1, lu, dup)
    ring1(2)
    for cp in downs:
        cp.wait_recv()
    relay(dm, rdm, m_send.at[2], m_recv.at[2])
    ring2(0)
    mids_here(0, lg, dgate)
    mids_here(1, lu, dup)
    ring2(1)

    await_bytes(rdm.at[:, :, pl.ds(0, 480)], m_recv.at[2])
    ring1(4)
    for h in range(2):
        out_v[h * HALF:(h + 1) * HALF, :] = (
            dot(ldt[:, 0:512], rdm[0, h]) + dot(ldt[:, 512:], rdm[1, h])
        ).T.astype(BF)
    store(out_v, out_o)

    for cp in crossing:
        cp.wait_recv()

    def stacked(h, b):
        rows = rows_at(b, KW)
        return jnp.concatenate([back[y, gu, h, rows, :] for y in range(2) for gu in range(2)], axis=0)

    def dx_part(h, zz, c):
        b = zz * 2 + c
        return dot(stacked(h, b), columns(b, 0, 1), TN)

    def for_sibling(d):
        zz = (z + 4 + d) % 8
        for h in range(2):
            lgt[h * 8 + zz] = dx_part(h, zz, 1 - core).astype(BF)
            pltpu.make_async_remote_copy(
                src_ref=lgt.at[h * 8 + zz], dst_ref=sums_in.at[h, zz], send_sem=s_send.at[0], recv_sem=s_recv.at[h, d],
                device_id=(dp, sibling), device_id_type=MESH,
            ).start()

    for d in range(8):
        for_sibling(d)

    def slab_sum(h, off):
        zz = (z + off) % 8
        await_bytes(sums_in.at[h, zz], s_recv.at[h, (off + 4) % 8])
        return dx_part(h, zz, core) + sums_in[h, zz].astype(F32)

    REACH = ((4, 3), (3, 4))
    links = []

    def chain(d):
        for h in range(2):
            for way, (sign, to) in enumerate(((1, up_z), (-1, down_z))):
                far = REACH[h][way]
                if d > far:
                    continue
                v = slab_sum(h, sign * d)
                if d < far:
                    await_bytes(chain_in.at[h, way, d], ch_recv.at[h, way, d])
                    v = v + chain_in[h, way, d].astype(F32)
                slot = (h * 2 + way) * 4 + d - 1
                lut[slot] = v.astype(BF)
                cp = pltpu.make_async_remote_copy(
                    src_ref=lut.at[slot], dst_ref=chain_in.at[h, way, d - 1],
                    send_sem=ch_send.at[slot], recv_sem=ch_recv.at[h, way, d - 1],
                    device_id=(dp, to), device_id_type=MESH,
                )
                cp.start()
                links.append(cp)

    def part_in(b):
        return dot(stacked(0, b), xall[0, b]) + dot(stacked(1, b), xall[1, b])

    chain(4)
    ring1(3)
    chain(3)
    ring3(0)
    ring2(3)
    ring2(2)
    chain(2)
    ring3(1)
    chain(1)
    ring2(4)
    ring3(3)
    for h in range(2):
        v = slab_sum(h, 0)
        for way in range(2):
            await_bytes(chain_in.at[h, way, 0], ch_recv.at[h, way, 0])
            v = v + chain_in[h, way, 0].astype(F32)
        dx_v[h * HALF:(h + 1) * HALF, :] = v.astype(BF)
    store(dx_v, dx_o)
    ring4(0)
    ring4(1)

    ring4(3)
    final = []
    for par in range(2):
        for cs in range(2):
            to = (cs * 4 + ring // 4, yh * 16 + summed_block(dp, par))
            src, dst = wsum.at[pl.ds(par * 128 + cs * 64, 64)], wfin.at[ring % 4]
            away = pltpu.make_async_remote_copy(
                src_ref=src, dst_ref=dst, send_sem=wf_send.at[par * 2 + cs], recv_sem=wf_recv.at[0],
                device_id=to, device_id_type=MESH,
            )

            def keep(src=src, dst=dst):
                pltpu.make_async_copy(src, dst, wf_recv.at[0]).start()

            apart(*to, keep, away.start)
            final.append((to, away))
    ring3(2)
    ring3(4)
    await_bytes(wfin, wf_recv.at[0])
    for gu, (out, out_h) in enumerate(((rg_v, rg_o), (ru_v, ru_o))):
        out[...] = jnp.concatenate([wfin[j, gu * KW:(gu + 1) * KW, :] for j in range(4)], axis=0).T
        store(out, out_h.at[0])
    ring4(2)
    ring4(4)

    for h in range(2):
        await_bytes(xall.at[h, pl.ds(0, 15)], x_send.at[h])
    to_y.wait_send()
    await_bytes(rdd.at[:, :, pl.ds(0, 480)], d_send.at[1])
    await_bytes(wp.at[0, pl.ds(0, 15)], w_send.at[0])
    await_bytes(wp.at[pl.ds(0, 3)], w_send.at[1])
    await_bytes(rdm.at[:, :, pl.ds(0, 480)], m_send.at[2])
    for cp in crossing + links + downs:
        cp.wait_send()
    await_bytes(sums_in, s_send.at[0])
    for group in started:
        for cp in group:
            cp.wait_send()
    for to, away in final:
        apart(*to, lambda: None, away.wait_send)
    for cp in stores:
        cp.wait()


def hand_over(*refs):
    src, dst, held, (sem,) = refs[:8], refs[8:16], refs[16:24], refs[24:]
    arriving = [pltpu.make_async_copy(src[i], held[i], sem.at[0, i]) for i in range(8)]
    leaving = [pltpu.make_async_copy(held[i], dst[i], sem.at[1, i]) for i in range(8)]
    for cp in arriving:
        cp.start()
    for i in range(8):
        arriving[i].wait()
        leaving[i].start()
    for cp in leaving:
        cp.wait()


def per_device(tokens, gate_in, gate_out, up_in, up_out, down_in, down_out, cotangent):
    anyw = pl.BlockSpec(memory_space=pl.ANY)
    out_shape = (
        jax.ShapeDtypeStruct((TOK, DB), BF),
        jax.ShapeDtypeStruct((TOK, DB), BF),
        jax.ShapeDtypeStruct((1, DB, 128), BF),
        jax.ShapeDtypeStruct((1, 128, MB), BF),
        jax.ShapeDtypeStruct((1, DB, 128), BF),
        jax.ShapeDtypeStruct((1, 128, MB), BF),
        jax.ShapeDtypeStruct((1, 128, MB), BF),
        jax.ShapeDtypeStruct((1, 128, DB), BF),
    )
    V = pltpu.VMEM
    mids = V((2, MB, HALF), BF)
    wide = V((2, MB, HALF), F32)
    square = V((MB, MB), BF)
    dma = pltpu.SemaphoreType.DMA
    scratch = [
        V((TOK, DB), BF), V((TOK, DB), BF), V((DB, 128), BF), V((128, MB), BF),
        V((DB, 128), BF), V((128, MB), BF), V((128, MB), BF), V((128, DB), BF),
        V((2, 16, HALF, DB), BF), V((2, 512, DB), BF), V((4, 16, 2, 16, DB), BF), V((2, 2, 512, HALF), BF),
        V((DB, MB), BF), square, V((DB, MB), BF), square, square, V((MB, DB), BF), V((TOK, DB), BF),
        V((16, 256, 256), BF), V((16, 256, 256), BF), square, V((DB, MB), BF),
        V((2, 512, HALF), BF), V((2, 2, 512, HALF), BF), V((2, 2, 512, HALF), BF),
        V((2, 512, HALF), BF), V((2, 2, 512, HALF), BF), V((2, 2, 512, HALF), BF), V((2, 2, MB, HALF), BF),
        V((2, 2, 2, 512, HALF), BF), V((2, 8, HALF, DB), BF), V((2, 2, 4, HALF, DB), BF),
        wide, wide, mids, mids, mids,
        V((3, 2, 128, MB), BF), V((3, 2, 128, MB), BF), V((3, 2, 128, MB), BF), V((3, 128, MB), BF),
        V((3, 128, MB), BF), V((3, 128, MB), BF), V((3, 2, 128, MB), BF), V((3, 2, 128, MB), BF), V((3, 128, MB), BF),
        V((14, 256, DB), BF), V((14, 128, DB), BF), V((256, DB), F32), V((128, DB), F32), V((256, DB), BF), V((4, 64, DB), BF),
        dma((9,)), dma((8,)), dma((2,)), dma((2, 8)), dma((2, 8)), dma((2,)), dma((2,)), dma((2,)), dma((2,)),
        dma((2,)), dma((2,)),
        dma((3,)), dma((3,)), dma((25,)), dma((25,)),
        dma((2,)), dma((2,)), dma((1,)), dma((2, 8)), dma((16,)), dma((2, 2, 4)), dma((4,)), dma((1,)),
    ]
    results = pl.pallas_call(
        kernel,
        out_shape=out_shape,
        in_specs=[anyw] * 8,
        out_specs=(anyw,) * 8,
        scratch_shapes=scratch,
        compiler_params=pltpu.CompilerParams(
            collective_id=0, has_side_effects=True, vmem_limit_bytes=62 * 2**20
        ),
        cost_estimate=pl.CostEstimate(flops=12_000_000_000, bytes_accessed=10_000_000, transcendentals=1_000_000),
    )(tokens, gate_in, gate_out, up_in, up_out, down_in, down_out, cotangent)
    return pl.pallas_call(
        hand_over,
        out_shape=out_shape,
        in_specs=[anyw] * 8,
        out_specs=(anyw,) * 8,
        scratch_shapes=[V(o.shape, BF) for o in out_shape] + [pltpu.SemaphoreType.DMA((2, 8))],
    )(*results)


def solution(mesh):
    in_specs = (
        P("dp", "tensor"),
        P("tensor", None, None),
        P("tensor", None, None),
        P("tensor", None, None),
        P("tensor", None, None),
        P("tensor", None, None),
        P("tensor", None, None),
        P("dp", "tensor"),
    )
    out_specs = (
        P("dp", "tensor"),
        P("dp", "tensor"),
        P("tensor", None, "dp"),
        P("tensor", "dp", None),
        P("tensor", None, "dp"),
        P("tensor", "dp", None),
        P("tensor", "dp", None),
        P("tensor", "dp", None),
    )
    return jax.shard_map(
        per_device, mesh=mesh, in_specs=in_specs, out_specs=out_specs, check_vma=False
    )
```

```python
import jax
import jax.numpy as jnp
from jax import lax
from jax.experimental import pallas as pl
from jax.experimental.pallas import tpu as pltpu
from jax.sharding import PartitionSpec as P

MESH = pl.DeviceIdType.MESH
BF = jnp.bfloat16
F32 = jnp.float32
NT = (((1,), (1,)), ((), ()))
NN = (((1,), (0,)), ((), ()))
TN = (((0,), (0,)), ((), ()))
TOK, HALF, DB, MB, KW, NBLK, NDP = 512, 256, 256, 1024, 32, 32, 8


def dot(a, b, form=NN):
    return lax.dot_general(a, b, form, preferred_element_type=F32)


def rows_at(index, size):
    start = index * size
    return pl.ds(start if isinstance(start, int) else pl.multiple_of(start, size), size)


def tiles(count, body):
    def step(i, carry):
        body(i)
        return carry

    lax.fori_loop(0, count, step, 0)


def unrolled(count, body):
    for i in range(count):
        body(i)


def kernel(
    x_h, rg_h, lg_h, ru_h, lu_h, rd_h, ld_h, dy_h,
    out_o, dx_o, rg_o, lg_o, ru_o, lu_o, rd_o, ld_o,
    out_v, dx_v, rg_v, lg_v, ru_v, lu_v, rd_v, ld_v,
    xall, wt, wp, ps, rg, lg, ru, lu, rd, ld, dy,
    lgt, lut, rdt, ldt,
    dsend, dd, rdd, msend, dm, rdm, gum, back, sums_in, chain_in,
    gate, upper, hidden, dgate, dup,
    p2, pn, pp, ysend, ra, rb, rc, rdn, ye,
    wring, lring, wyout, wyin, lown, wsum, wfin,
    load_sem, store_sem, x_send, z_recv, c_recv, p_send, p_recv, d_send, d_recv, w_send, w_recv,
    m_send, m_recv, ring_send, ring_recv, cross_send, cross_recv,
    b_send, b_recv, s_send, s_recv, ch_send, ch_recv, wf_send, wf_recv,
):
    dp, tn = lax.axis_index("dp"), lax.axis_index("tensor")
    xc, yl = dp // 2, dp % 2
    yh, z, core = tn // 16, (tn // 2) % 8, tn % 2

    def block(y, zz, c):
        return (y * 8 + zz) * 2 + c

    def await_bytes(ref, sem):
        pltpu.make_async_copy(ref, ref, sem).wait()

    ring = z * 2 + core
    loads = {}
    for i, (name, src, dst) in enumerate((
        ("rg", rg_h.at[0], rg), ("ru", ru_h.at[0], ru),
        ("x0", x_h.at[pl.ds(0, HALF)], xall.at[0, ring]), ("x1", x_h.at[pl.ds(HALF, HALF)], xall.at[1, ring]),
        ("ld", ld_h.at[0], ld), ("dy", dy_h, dy), ("lg", lg_h.at[0], lg), ("lu", lu_h.at[0], lu), ("rd", rd_h.at[0], rd),
    )):
        loads[name] = pltpu.make_async_copy(src, dst, load_sem.at[i])
        loads[name].start()

    stores = []

    def store(src, dst):
        cp = pltpu.make_async_copy(src, dst, store_sem.at[len(stores)])
        cp.start()
        stores.append(cp)

    def peer(j):
        g = j // 4
        dz = 4 + (1 - 2 * (g % 2)) * ((g + 1) // 2)
        return block((yh + 1 - (j // 2) % 2) % 2, (z + dz) % 8, (core + 1 - j % 2) % 2)

    def dp_peer(j):
        return (dp + 2 * j + 2) % NDP

    barrier = pltpu.get_barrier_semaphore()

    def greet_tensor(j):
        pl.semaphore_signal(barrier, inc=1, device_id=(dp, peer(j)), device_id_type=MESH)

    def greet_dp(j):
        pl.semaphore_signal(barrier, inc=1, device_id=(dp_peer(j), tn), device_id_type=MESH)

    tiles(NBLK - 1, greet_tensor)
    tiles(3, greet_dp)
    pl.semaphore_signal(barrier, inc=1, device_id=(xc * 2 + 1 - yl, tn), device_id_type=MESH)

    def apart(to_dp, to_tn, here, there):
        same = jnp.logical_and(to_dp == dp, to_tn == tn)
        pl.when(same)(here)
        pl.when(jnp.logical_not(same))(there)

    def summed_block(d, par):
        return ((z + d + par * (8 - 2 * d)) % 8) * 2 + par

    for j in range(4):
        away = 8 + z - (2 * (dp % 4) + j // 2)
        source = ((away * (1 + 6 * core)) % 8, yh * 16 + 4 * (dp % 4) + j)

        def greet_source(source=source):
            pl.semaphore_signal(barrier, inc=1, device_id=source, device_id_type=MESH)

        apart(*source, lambda: None, greet_source)
    stays = jnp.logical_and(dp == 0, z < 2).astype(jnp.int32)

    OFFS = ((0, -1, 1, -2, 2, -3, 3, -4), (0, -1, 1, -2, 2, -3, 3, 4))

    def x_copy(h, b, sem, to):
        pltpu.make_async_remote_copy(
            src_ref=xall.at[h, b], dst_ref=xall.at[h, b], send_sem=x_send.at[h], recv_sem=sem,
            device_id=(dp, to), device_id_type=MESH,
        ).start()

    up_z, down_z = block(yh, (z + 1) % 8, core), block(yh, (z + 7) % 8, core)
    over_y, sibling = block(1 - yh, z, core), block(yh, z, 1 - core)

    def z_event(h, k):
        off = OFFS[h][k]
        b = ((z + off) % 8) * 2 + core
        if k:
            await_bytes(xall.at[h, b], z_recv.at[h, k])
        for sign, to in ((-1, up_z), (1, down_z)):
            if (off == 0 or off * sign > 0) and off + sign in OFFS[h]:
                x_copy(h, b, z_recv.at[h, OFFS[h].index(off + sign)], to)
        x_copy(h, b, c_recv.at[h, k], sibling)

    def flip(src, dst, across, r):
        def body(c):
            dst[rows_at(c, 256), pl.ds(r * 256, 256)] = src[pl.ds(r * 256, 256), rows_at(c, 256)].T

        tiles(across, body)

    loads["rg"].wait()
    loads["ru"].wait()

    @pl.when(xc < 2)
    def _():
        for r in range(4):
            wt[r // 2, pl.ds(r % 2 * 256, 256), :] = rg[:, pl.ds(r * 256, 256)].T

    @pl.when(xc >= 2)
    def _():
        for r in range(4):
            wt[r // 2, pl.ds(r % 2 * 256, 256), :] = ru[:, pl.ds(r * 256, 256)].T

    def w_rows(at):
        return pl.ds(pl.multiple_of(at * KW + (xc % 2) * 16, 16), 16)

    def send_w(j):
        at = (ring + 1 + j) % 16
        pltpu.make_async_remote_copy(
            src_ref=wt.at[:, w_rows(at)], dst_ref=wp.at[xc, ring], send_sem=w_send.at[0], recv_sem=w_recv.at[0],
            device_id=(dp, yh * 16 + at), device_id_type=MESH,
        ).start()

    pl.semaphore_wait(barrier, NBLK - 1 + 3 + 1 + 4 - stays)
    tiles(15, send_w)
    loads["x0"].wait()
    z_event(0, 0)
    loads["x1"].wait()
    z_event(1, 0)
    wp[xc, ring] = wt[:, w_rows(ring), :]

    loads["dy"].wait()
    loads["ld"].wait()

    def back_down(q):
        rows = rows_at(q, 256)
        for h in range(2):
            toks = dy[h * HALF:(h + 1) * HALF, :]
            dsend[h, rows, :] = dot(ld[pl.ds(pl.multiple_of((1 - yh) * 512 + q * 256, 256), 256), :], toks, NT).astype(BF)
            dd[yh, h, rows, :] = dot(ld[pl.ds(pl.multiple_of(yh * 512 + q * 256, 256), 256), :], toks, NT).astype(BF)

    tiles(2, back_down)
    to_y = pltpu.make_async_remote_copy(
        src_ref=dsend, dst_ref=dd.at[yh], send_sem=d_send.at[0], recv_sem=d_recv.at[0],
        device_id=(dp, over_y), device_id_type=MESH,
    )
    to_y.start()

    HOPS = (8, 7, 9, 6, 10, 5, 11, 12, 4, 13, 3, 14, 2, 15, 1)

    def relay(held, dst, send_sem, recv_sem, start=0, end=15, h=slice(None)):
        for hop in HOPS[start:end]:
            at = (ring + hop) % 16
            pltpu.make_async_remote_copy(
                src_ref=held.at[:, h, rows_at(at, KW)], dst_ref=dst.at[:, h, rows_at(ring, KW)],
                send_sem=send_sem, recv_sem=recv_sem, device_id=(dp, yh * 16 + at), device_id_type=MESH,
            ).start()
        if end == 15:
            dst[:, h, rows_at(ring, KW), :] = held[:, h, rows_at(ring, KW), :]

    def flip_blocks(src, dst):
        def body(i):
            r, c = i // 4, i % 4
            dst[c * 4 + r] = src[rows_at(r, 256), rows_at(c, 256)].T

        tiles(16, body)

    def block_row(t, q):
        return jnp.concatenate([t[q * 4 + c] for c in range(4)], axis=1)

    loads["lg"].wait()
    flip_blocks(lg, lgt)

    await_bytes(wp.at[0, pl.ds(0, 15)], w_recv.at[0])

    def share_w(j):
        to = ((xc + 1 + j) % 4) * 2 + yl
        pltpu.make_async_remote_copy(
            src_ref=wp.at[xc], dst_ref=wp.at[xc], send_sem=w_send.at[1], recv_sem=w_recv.at[1],
            device_id=(to, tn), device_id_type=MESH,
        ).start()

    tiles(3, share_w)

    def columns(b, *ys):
        return jnp.concatenate([wp[p, b, y] for y in ys for p in range(4)], axis=0)

    def first(h, *ks):
        for k in ks:
            await_bytes(xall.at[h, 0], c_recv.at[h, k])
            at = (z + OFFS[h][k]) % 8

            def body(c, at=at):
                b = at * 2 + c
                w = columns(b, yh, 1 - yh)
                v = dot(w, xall[h, b], NT).astype(BF)
                own, rows = rows_at(yh * 16 + b, KW), rows_at(b, KW)
                gum[h, 0, own, :] = v[0:32]
                gum[h, 1, own, :] = v[32:64]
                ps[h, 0, rows, :] = v[64:96]
                ps[h, 1, rows, :] = v[96:128]
                pltpu.make_async_remote_copy(
                    src_ref=ps.at[h, :, rows], dst_ref=gum.at[h, :, own], send_sem=p_send.at[h], recv_sem=p_recv.at[h],
                    device_id=(dp, over_y), device_id_type=MESH,
                ).start()

            tiles(2, body)

    def events(h, *ks):
        for k in ks:
            z_event(h, k)

    loads["lu"].wait()
    flip_blocks(lu, lut)
    events(0, 1, 2)
    events(1, 1, 2)
    loads["rd"].wait()
    for r in range(4):
        flip(rd, rdt, 4, r)
    events(0, 3, 4)
    events(1, 3, 4)
    for r in range(4):
        flip(ld, ldt, 1, r)
    await_bytes(wp.at[pl.ds(0, 3)], w_recv.at[1])
    first(0, 0, 1, 2, 3, 4)
    events(0, 5, 6)
    events(1, 5, 6)
    to_y.wait_recv()
    relay(dd, rdd, d_send.at[1], d_recv.at[1], 0, 4)
    first(0, 5, 6)
    first(1, 0, 1, 2)
    events(0, 7)
    events(1, 7)
    relay(dd, rdd, d_send.at[1], d_recv.at[1], 4, 15)
    first(0, 7)
    first(1, 3, 4, 5, 6, 7)

    downs = []

    def forward(h):
        await_bytes(gum.at[h, :, pl.ds(0, 512)], p_recv.at[h])

        def body(q):
            rows = rows_at(q, 256)
            g = dot(block_row(lgt, q), gum[h, 0])
            u = dot(block_row(lut, q), gum[h, 1])
            gate[h, rows, :] = g
            upper[h, rows, :] = u
            hidden[h, rows, :] = (g * jax.nn.sigmoid(g) * u).astype(BF)

        unrolled(4, body)

        def down_over(q):
            rows = pl.ds(pl.multiple_of((1 - yh) * 512 + q * 256, 256), 256)
            msend[h, rows_at(q, 256), :] = dot(rdt[rows, :], hidden[h]).astype(BF)

        unrolled(2, down_over)
        cp = pltpu.make_async_remote_copy(
            src_ref=msend.at[h], dst_ref=dm.at[yh, h], send_sem=m_send.at[h], recv_sem=m_recv.at[h],
            device_id=(dp, over_y), device_id_type=MESH,
        )
        cp.start()
        downs.append(cp)

        def down_here(q):
            rows = pl.ds(pl.multiple_of(yh * 512 + q * 256, 256), 256)
            dm[yh, h, rows_at(q, 256), :] = dot(rdt[rows, :], hidden[h]).astype(BF)

        unrolled(2, down_here)

    forward(0)
    forward(1)
    await_bytes(rdd.at[:, :, pl.ds(0, 480)], d_recv.at[1])

    def backward(h):
        def body(q):
            rows = rows_at(q, 256)
            dh = dot(rd[rows, 0:512], rdd[0, h]) + dot(rd[rows, 512:1024], rdd[1, h])
            g, u = gate[h, rows, :], upper[h, rows, :]
            s = jax.nn.sigmoid(g)
            dgate[h, rows, :] = (dh * u * s * (1.0 + g * (1.0 - s))).astype(BF)
            dup[h, rows, :] = (dh * (g * s)).astype(BF)

        unrolled(4, body)

    nxt, prv, opp = (xc + 1) % 4, (xc + 3) % 4, (xc + 2) % 4

    def ship(src, dst, sem, to):
        cp = pltpu.make_async_remote_copy(
            src_ref=src, dst_ref=dst, send_sem=ring_send.at[sem], recv_sem=ring_recv.at[sem],
            device_id=to, device_id_type=MESH,
        )
        cp.start()
        return cp

    to_next, to_prev = (nxt * 2 + yl, tn), (prv * 2 + yl, tn)
    to_pair = (xc * 2 + 1 - yl, tn)
    big = (
        (hidden, rdd, rd_v, rd_o),
        (gum.at[:, 0], dgate, lg_v, lg_o),
        (gum.at[:, 1], dup, lu_v, lu_o),
    )

    def part(a, q, half):
        if a == 3:
            return part_in(summed_block(2 * q + yl, half)) + wyin[q, half].astype(F32)
        if a == 4:
            rows = pl.ds(pl.multiple_of(q % 2 * 256 + half * 128, 128), 128)
            return dot(rdm[q // 2, 0, rows, :], dy[0:HALF, :]) + dot(rdm[q // 2, 1, rows, :], dy[HALF:, :])
        rows = pl.ds(pl.multiple_of(q * 256 + half * 128, 128), 128)
        if a in (2, 5):
            cols = slice(0, 512) if a == 2 else slice(512, 1024)
            return dot(gum[0, 1, rows, :], dup[0, cols, :], NT) + dot(gum[1, 1, rows, :], dup[1, cols, :], NT)
        left, right = big[a][:2]

        def both(pick):
            return dot(left[0, rows, :], pick(0), NT) + dot(left[1, rows, :], pick(1), NT)

        if a == 0:
            return jnp.concatenate([both(lambda h, y=y: rdd[y, h]) for y in range(2)], axis=1)
        return both(lambda h: right[h])

    started = [[None] * 5 for _ in range(6)]
    steps = (p2, pn, pp, ysend, ra, rb, rc, rdn, ye)
    places = [tuple(ref.at[a] for ref in steps) for a in range(2)]

    def columns_of(a):
        at = pl.ds(0 if a == 2 else 512, 512)
        return tuple(ref.at[2, :, :, at] if ref.ndim == 4 else ref.at[2, :, at] for ref in steps)

    places.append(columns_of(2))
    for ref in (wring, lring):
        places.append(tuple(
            ref.at[at] if size == 1 else ref.at[pl.ds(at, size)]
            for at, size in ((0, 2), (2, 2), (4, 2), (6, 1), (7, 1), (8, 1), (9, 2), (11, 2), (13, 1))
        ))
    places.append(columns_of(5))

    crossed = []

    def cross_first():
        for n, q in enumerate((opp, nxt, prv, xc)):
            for half in range(2):
                wyout[q, half] = part_in(summed_block(2 * q + 1 - yl, half)).astype(BF)
            cp = pltpu.make_async_remote_copy(
                src_ref=wyout.at[q], dst_ref=wyin.at[q], send_sem=cross_send.at[n], recv_sem=cross_recv.at[n],
                device_id=to_pair, device_id_type=MESH,
            )
            cp.start()
            crossed.append(cp)

    def ring1(a):
        p2, _, _, _, ra, rb = places[a][:6]
        if a == 3:
            crossed[0].wait_recv()

        def put(half):
            p2[half] = part(a, opp, half).astype(BF)

        tiles(2, put)
        started[a][0] = ship(p2.at[0], ra, 5 * a, to_next)
        started[a][1] = ship(p2.at[1], rb, 5 * a + 1, to_prev)

    def ring2(a):
        _, pn, pp, _, ra, rb, rc, rdn, _ = places[a]
        if a == 3:
            crossed[1].wait_recv()
            crossed[2].wait_recv()

        def put_n(half):
            pn[half] = part(a, nxt, half).astype(BF)

        def put_p(half):
            pp[half] = part(a, prv, half).astype(BF)

        tiles(2, put_n)
        started[a][0].wait_recv()
        pn[0] = (pn[0].astype(F32) + ra[...].astype(F32)).astype(BF)
        started[a][2] = ship(pn, rc, 5 * a + 2, to_next)
        tiles(2, put_p)
        started[a][1].wait_recv()
        pp[1] = (pp[1].astype(F32) + rb[...].astype(F32)).astype(BF)
        started[a][3] = ship(pp, rdn, 5 * a + 3, to_prev)

    def kept(a, c):
        return c % 2, pl.ds((a * 2 + c // 2) * 128, 128)

    def ring3(a):
        _, _, _, ysend, _, _, rc, rdn, ye = places[a]
        if a == 3:
            crossed[3].wait_recv()
        started[a][2].wait_recv()
        started[a][3].wait_recv()

        def total(half):
            return part(a, xc, half) + rc[half].astype(F32) + rdn[half].astype(F32)

        if a == 3:
            for half in range(2):
                wsum[half * 128:(half + 1) * 128, :] = total(half).astype(BF)
            return
        ysend[...] = total(1 - yl).astype(BF)
        started[a][4] = ship(ysend, ye, 5 * a + 4, to_pair)
        own = total(yl)
        if a == 4:
            lown[...] = own
            return
        for c, cols in wide_columns(a):
            s, rows = kept(min(a, 2), c)
            upper[s, rows, :] = own[:, cols]

    def wide_columns(a):
        first = 2 if a == 5 else 0
        return [(first + c, slice(c * 256, (c + 1) * 256)) for c in range(2 if a in (2, 5) else 4)]

    def ring4(a):
        ye = places[a][8]
        started[a][4].wait_recv()
        if a == 4:
            ld_v[...] = (lown[...] + ye[...].astype(F32)).astype(BF)
            store(ld_v, ld_o.at[0])
            return
        out, out_h = big[min(a, 2)][2:]
        for c, cols in wide_columns(a):
            s, rows = kept(min(a, 2), c)
            out[:, c * 256:(c + 1) * 256] = (upper[s, rows, :] + ye[:, cols].astype(F32)).astype(BF)
        if a != 2:
            store(out, out_h.at[0])

    for h in range(2):
        await_bytes(ps.at[h], p_send.at[h])
    crossing = []

    def mids_over(gu, h):
        w, d = ((lg, dgate), (lu, dup))[gu]
        for q in range(2):
            src = pl.ds(pl.multiple_of((1 - yh) * 512 + q * 256, 256), 256)
            ps[gu, h, q * 256:(q + 1) * 256, :] = dot(w[src, :], d[h]).astype(BF)
        cp = pltpu.make_async_remote_copy(
            src_ref=ps.at[gu, h], dst_ref=back.at[yh, gu, h], send_sem=b_send.at[gu * 2 + h], recv_sem=b_recv.at[gu * 2 + h],
            device_id=(dp, over_y), device_id_type=MESH,
        )
        cp.start()
        crossing.append(cp)

    def mids_here(gu, h):
        w, d = ((lg, dgate), (lu, dup))[gu]
        for q in range(2):
            src = pl.ds(pl.multiple_of(yh * 512 + q * 256, 256), 256)
            back[yh, gu, h, q * 256:(q + 1) * 256, :] = dot(w[src, :], d[h]).astype(BF)

    downs[0].wait_recv()
    relay(dm, rdm, m_send.at[2], m_recv.at[2], 0, 15, 0)
    ring1(0)
    backward(0)
    mids_over(0, 0)
    mids_over(1, 0)
    backward(1)
    mids_over(0, 1)
    mids_over(1, 1)
    ring1(1)
    downs[1].wait_recv()
    relay(dm, rdm, m_send.at[3], m_recv.at[3], 0, 7, 1)
    ring1(2)
    ring1(5)
    mids_here(0, 0)
    mids_here(1, 0)
    ring2(0)
    mids_here(0, 1)
    mids_here(1, 1)
    ring2(1)

    def outputs():
        for h in range(2):
            await_bytes(rdm.at[:, h, pl.ds(0, 480)], m_recv.at[2 + h])
        ring1(4)
        for h in range(2):
            out_v[h * HALF:(h + 1) * HALF, :] = (
                dot(ldt[:, 0:512], rdm[0, h]) + dot(ldt[:, 512:], rdm[1, h])
            ).T.astype(BF)
        store(out_v, out_o)

    def stacked(h, b):
        rows = rows_at(b, KW)
        return jnp.concatenate([back[y, gu, h, rows, :] for y in range(2) for gu in range(2)], axis=0)

    def dx_part(h, zz, c):
        b = zz * 2 + c
        return dot(stacked(h, b), columns(b, 0, 1), TN)

    def for_sibling(h):
        for cp in crossing[2 * h:2 * h + 2]:
            cp.wait_recv()
        for d in range(8):
            zz = (z + 4 + d) % 8
            lgt[h * 8 + zz] = dx_part(h, zz, 1 - core).astype(BF)
            pltpu.make_async_remote_copy(
                src_ref=lgt.at[h * 8 + zz], dst_ref=sums_in.at[h, zz], send_sem=s_send.at[0], recv_sem=s_recv.at[h, d],
                device_id=(dp, sibling), device_id_type=MESH,
            ).start()

    def slab_sum(h, off):
        zz = (z + off) % 8
        await_bytes(sums_in.at[h, zz], s_recv.at[h, (off + 4) % 8])
        return dx_part(h, zz, core) + sums_in[h, zz].astype(F32)

    REACH = ((4, 3), (3, 4))
    links = []

    def chain(d, h):
        for way, (sign, to) in enumerate(((1, up_z), (-1, down_z))):
            far = REACH[h][way]
            if d > far:
                continue
            v = slab_sum(h, sign * d)
            if d < far:
                await_bytes(chain_in.at[h, way, d], ch_recv.at[h, way, d])
                v = v + chain_in[h, way, d].astype(F32)
            slot = (h * 2 + way) * 4 + d - 1
            lut[slot] = v.astype(BF)
            cp = pltpu.make_async_remote_copy(
                src_ref=lut.at[slot], dst_ref=chain_in.at[h, way, d - 1],
                send_sem=ch_send.at[slot], recv_sem=ch_recv.at[h, way, d - 1],
                device_id=(dp, to), device_id_type=MESH,
            )
            cp.start()
            links.append(cp)

    def part_in(b):
        return dot(stacked(0, b), xall[0, b]) + dot(stacked(1, b), xall[1, b])

    def tokens_grad(h):
        v = slab_sum(h, 0)
        for way in range(2):
            await_bytes(chain_in.at[h, way, 0], ch_recv.at[h, way, 0])
            v = v + chain_in[h, way, 0].astype(F32)
        dx_v[h * HALF:(h + 1) * HALF, :] = v.astype(BF)

    for_sibling(0)
    chain(4, 0)
    chain(3, 0)
    for_sibling(1)
    chain(4, 1)
    cross_first()
    chain(2, 0)
    relay(dm, rdm, m_send.at[3], m_recv.at[3], 7, 15, 1)
    ring1(3)
    ring2(2)
    ring3(0)
    chain(3, 1)
    ring2(3)
    outputs()
    ring2(5)
    chain(1, 0)
    ring3(1)
    chain(2, 1)

    ring3(3)
    final = []
    for par in range(2):
        for cs in range(2):
            to = (cs * 4 + ring // 4, yh * 16 + summed_block(dp, par))
            src, dst = wsum.at[pl.ds(par * 128 + cs * 64, 64)], wfin.at[ring % 4]
            away = pltpu.make_async_remote_copy(
                src_ref=src, dst_ref=dst, send_sem=wf_send.at[par * 2 + cs], recv_sem=wf_recv.at[0],
                device_id=to, device_id_type=MESH,
            )

            def keep(src=src, dst=dst):
                pltpu.make_async_copy(src, dst, wf_recv.at[0]).start()

            apart(*to, keep, away.start)
            final.append((to, away))
    ring3(2)
    ring2(4)
    tokens_grad(0)
    chain(1, 1)
    ring4(0)
    ring3(5)
    ring3(4)
    ring4(1)
    tokens_grad(1)
    store(dx_v, dx_o)
    ring4(2)
    ring4(5)
    await_bytes(wfin, wf_recv.at[0])
    for gu, (out, out_h) in enumerate(((rg_v, rg_o), (ru_v, ru_o))):
        out[...] = jnp.concatenate([wfin[j, gu * KW:(gu + 1) * KW, :] for j in range(4)], axis=0).T
        store(out, out_h.at[0])
    ring4(4)

    for h in range(2):
        await_bytes(xall.at[h, pl.ds(0, 15)], x_send.at[h])
    to_y.wait_send()
    await_bytes(rdd.at[:, :, pl.ds(0, 480)], d_send.at[1])
    await_bytes(wp.at[0, pl.ds(0, 15)], w_send.at[0])
    await_bytes(wp.at[pl.ds(0, 3)], w_send.at[1])
    for h in range(2):
        await_bytes(rdm.at[:, h, pl.ds(0, 480)], m_send.at[2 + h])
    for cp in crossing + links + downs:
        cp.wait_send()
    await_bytes(sums_in, s_send.at[0])
    for group in started + [crossed]:
        for cp in group:
            if cp is not None:
                cp.wait_send()
    for to, away in final:
        apart(*to, lambda: None, away.wait_send)
    for cp in stores:
        cp.wait()


def hand_over(*refs):
    src, dst, held, (sem,) = refs[:8], refs[8:16], refs[16:24], refs[24:]
    arriving = [pltpu.make_async_copy(src[i], held[i], sem.at[0, i]) for i in range(8)]
    leaving = [pltpu.make_async_copy(held[i], dst[i], sem.at[1, i]) for i in range(8)]
    for cp in arriving:
        cp.start()
    for i in range(8):
        arriving[i].wait()
        leaving[i].start()
    for cp in leaving:
        cp.wait()


def per_device(tokens, gate_in, gate_out, up_in, up_out, down_in, down_out, cotangent):
    anyw = pl.BlockSpec(memory_space=pl.ANY)
    out_shape = (
        jax.ShapeDtypeStruct((TOK, DB), BF),
        jax.ShapeDtypeStruct((TOK, DB), BF),
        jax.ShapeDtypeStruct((1, DB, 128), BF),
        jax.ShapeDtypeStruct((1, 128, MB), BF),
        jax.ShapeDtypeStruct((1, DB, 128), BF),
        jax.ShapeDtypeStruct((1, 128, MB), BF),
        jax.ShapeDtypeStruct((1, 128, MB), BF),
        jax.ShapeDtypeStruct((1, 128, DB), BF),
    )
    V = pltpu.VMEM
    mids = V((2, MB, HALF), BF)
    wide = V((2, MB, HALF), F32)
    square = V((MB, MB), BF)
    dma = pltpu.SemaphoreType.DMA
    scratch = [
        V((TOK, DB), BF), V((TOK, DB), BF), V((DB, 128), BF), V((128, MB), BF),
        V((DB, 128), BF), V((128, MB), BF), V((128, MB), BF), V((128, DB), BF),
        V((2, 16, HALF, DB), BF), V((2, 512, DB), BF), V((4, 16, 2, 16, DB), BF), V((2, 2, 512, HALF), BF),
        V((DB, MB), BF), square, V((DB, MB), BF), square, square, V((MB, DB), BF), V((TOK, DB), BF),
        V((16, 256, 256), BF), V((16, 256, 256), BF), square, V((DB, MB), BF),
        V((2, 512, HALF), BF), V((2, 2, 512, HALF), BF), V((2, 2, 512, HALF), BF),
        V((2, 512, HALF), BF), V((2, 2, 512, HALF), BF), V((2, 2, 512, HALF), BF), V((2, 2, MB, HALF), BF),
        V((2, 2, 2, 512, HALF), BF), V((2, 8, HALF, DB), BF), V((2, 2, 4, HALF, DB), BF),
        wide, wide, mids, mids, mids,
        V((3, 2, 128, MB), BF), V((3, 2, 128, MB), BF), V((3, 2, 128, MB), BF), V((3, 128, MB), BF),
        V((3, 128, MB), BF), V((3, 128, MB), BF), V((3, 2, 128, MB), BF), V((3, 2, 128, MB), BF), V((3, 128, MB), BF),
        V((14, 128, DB), BF), V((14, 128, DB), BF), V((4, 2, 128, DB), BF), V((4, 2, 128, DB), BF),
        V((128, DB), F32), V((256, DB), BF), V((4, 64, DB), BF),
        dma((9,)), dma((8,)), dma((2,)), dma((2, 8)), dma((2, 8)), dma((2,)), dma((2,)), dma((2,)), dma((2,)),
        dma((2,)), dma((2,)),
        dma((4,)), dma((4,)), dma((30,)), dma((30,)), dma((4,)), dma((4,)),
        dma((4,)), dma((4,)), dma((1,)), dma((2, 8)), dma((16,)), dma((2, 2, 4)), dma((4,)), dma((1,)),
    ]
    results = pl.pallas_call(
        kernel,
        out_shape=out_shape,
        in_specs=[anyw] * 8,
        out_specs=(anyw,) * 8,
        scratch_shapes=scratch,
        compiler_params=pltpu.CompilerParams(
            collective_id=0, has_side_effects=True, vmem_limit_bytes=62 * 2**20
        ),
        cost_estimate=pl.CostEstimate(flops=12_000_000_000, bytes_accessed=10_000_000, transcendentals=1_000_000),
    )(tokens, gate_in, gate_out, up_in, up_out, down_in, down_out, cotangent)
    return pl.pallas_call(
        hand_over,
        out_shape=out_shape,
        in_specs=[anyw] * 8,
        out_specs=(anyw,) * 8,
        scratch_shapes=[V(o.shape, BF) for o in out_shape] + [pltpu.SemaphoreType.DMA((2, 8))],
    )(*results)


def solution(mesh):
    in_specs = (
        P("dp", "tensor"),
        P("tensor", None, None),
        P("tensor", None, None),
        P("tensor", None, None),
        P("tensor", None, None),
        P("tensor", None, None),
        P("tensor", None, None),
        P("dp", "tensor"),
    )
    out_specs = (
        P("dp", "tensor"),
        P("dp", "tensor"),
        P("tensor", None, "dp"),
        P("tensor", "dp", None),
        P("tensor", None, "dp"),
        P("tensor", "dp", None),
        P("tensor", "dp", None),
        P("tensor", "dp", None),
    )
    return jax.shard_map(
        per_device, mesh=mesh, in_specs=in_specs, out_specs=out_specs, check_vma=False
    )
```

```python
import jax
import jax.numpy as jnp
from jax import lax
from jax.experimental import pallas as pl
from jax.experimental.pallas import tpu as pltpu
from jax.sharding import PartitionSpec as P

MESH = pl.DeviceIdType.MESH
BF = jnp.bfloat16
F32 = jnp.float32
NT = (((1,), (1,)), ((), ()))
NN = (((1,), (0,)), ((), ()))
TN = (((0,), (0,)), ((), ()))
TOK, HALF, DB, MB, KW, NBLK, NDP = 512, 256, 256, 1024, 32, 32, 8


def dot(a, b, form=NN):
    return lax.dot_general(a, b, form, preferred_element_type=F32)


def rows_at(index, size):
    start = index * size
    return pl.ds(start if isinstance(start, int) else pl.multiple_of(start, size), size)


def tiles(count, body):
    def step(i, carry):
        body(i)
        return carry

    lax.fori_loop(0, count, step, 0)


def unrolled(count, body):
    for i in range(count):
        body(i)


def kernel(
    x_h, rg_h, lg_h, ru_h, lu_h, rd_h, ld_h, dy_h,
    out_o, dx_o, rg_o, lg_o, ru_o, lu_o, rd_o, ld_o,
    out_v, dx_v, rg_v, lg_v, ru_v, lu_v, rd_v, ld_v,
    xall, wt, wp, ps, rg, lg, ru, lu, rd, ld, dy,
    lgt, lut, rdt, ldt,
    dsend, dd, rdd, msend, dm, rdm, gum, back, sums_in, chain_in,
    gate, upper, hidden, dgate, dup,
    p2, pn, pp, ysend, ra, rb, rc, rdn, ye,
    wring, lring, wyout, wyin, lown, wsum, wfin,
    load_sem, store_sem, x_send, z_recv, c_recv, p_send, p_recv, d_send, d_recv, w_send, w_recv,
    m_send, m_recv, ring_send, ring_recv, cross_send, cross_recv,
    b_send, b_recv, s_send, s_recv, ch_send, ch_recv, wf_send, wf_recv,
):
    dp, tn = lax.axis_index("dp"), lax.axis_index("tensor")
    xc, yl = dp // 2, dp % 2
    yh, z, core = tn // 16, (tn // 2) % 8, tn % 2

    def block(y, zz, c):
        return (y * 8 + zz) * 2 + c

    def await_bytes(ref, sem):
        pltpu.make_async_copy(ref, ref, sem).wait()

    ring = z * 2 + core
    loads = {}
    for i, (name, src, dst) in enumerate((
        ("rg", rg_h.at[0], rg), ("ru", ru_h.at[0], ru),
        ("x0", x_h.at[pl.ds(0, HALF)], xall.at[0, ring]), ("x1", x_h.at[pl.ds(HALF, HALF)], xall.at[1, ring]),
        ("ld", ld_h.at[0], ld), ("dy", dy_h, dy), ("lg", lg_h.at[0], lg), ("lu", lu_h.at[0], lu), ("rd", rd_h.at[0], rd),
    )):
        loads[name] = pltpu.make_async_copy(src, dst, load_sem.at[i])
        loads[name].start()

    stores = []

    def store(src, dst):
        cp = pltpu.make_async_copy(src, dst, store_sem.at[len(stores)])
        cp.start()
        stores.append(cp)

    def peer(j):
        g = j // 4
        dz = 4 + (1 - 2 * (g % 2)) * ((g + 1) // 2)
        return block((yh + 1 - (j // 2) % 2) % 2, (z + dz) % 8, (core + 1 - j % 2) % 2)

    def dp_peer(j):
        return (dp + 2 * j + 2) % NDP

    barrier = pltpu.get_barrier_semaphore()

    def greet_tensor(j):
        pl.semaphore_signal(barrier, inc=1, device_id=(dp, peer(j)), device_id_type=MESH)

    def greet_dp(j):
        pl.semaphore_signal(barrier, inc=1, device_id=(dp_peer(j), tn), device_id_type=MESH)

    tiles(NBLK - 1, greet_tensor)
    tiles(3, greet_dp)
    pl.semaphore_signal(barrier, inc=1, device_id=(xc * 2 + 1 - yl, tn), device_id_type=MESH)

    def apart(to_dp, to_tn, here, there):
        same = jnp.logical_and(to_dp == dp, to_tn == tn)
        pl.when(same)(here)
        pl.when(jnp.logical_not(same))(there)

    def summed_block(d, par):
        return ((z + d + par * (8 - 2 * d)) % 8) * 2 + par

    for j in range(4):
        away = 8 + z - (2 * (dp % 4) + j // 2)
        source = ((away * (1 + 6 * core)) % 8, yh * 16 + 4 * (dp % 4) + j)

        def greet_source(source=source):
            pl.semaphore_signal(barrier, inc=1, device_id=source, device_id_type=MESH)

        apart(*source, lambda: None, greet_source)
    stays = jnp.logical_and(dp == 0, z < 2).astype(jnp.int32)

    OFFS = ((0, -1, 1, -2, 2, -3, 3, -4), (0, -1, 1, -2, 2, -3, 3, 4))

    def x_copy(h, b, sem, to):
        pltpu.make_async_remote_copy(
            src_ref=xall.at[h, b], dst_ref=xall.at[h, b], send_sem=x_send.at[h], recv_sem=sem,
            device_id=(dp, to), device_id_type=MESH,
        ).start()

    up_z, down_z = block(yh, (z + 1) % 8, core), block(yh, (z + 7) % 8, core)
    over_y, sibling = block(1 - yh, z, core), block(yh, z, 1 - core)

    def z_event(h, k):
        off = OFFS[h][k]
        b = ((z + off) % 8) * 2 + core
        if k:
            await_bytes(xall.at[h, b], z_recv.at[h, k])
        for sign, to in ((-1, up_z), (1, down_z)):
            if (off == 0 or off * sign > 0) and off + sign in OFFS[h]:
                x_copy(h, b, z_recv.at[h, OFFS[h].index(off + sign)], to)
        x_copy(h, b, c_recv.at[h, k], sibling)

    def flip(src, dst, across, r):
        def body(c):
            dst[rows_at(c, 256), pl.ds(r * 256, 256)] = src[pl.ds(r * 256, 256), rows_at(c, 256)].T

        tiles(across, body)

    loads["rg"].wait()
    loads["ru"].wait()

    @pl.when(xc < 2)
    def _():
        for r in range(4):
            wt[r // 2, pl.ds(r % 2 * 256, 256), :] = rg[:, pl.ds(r * 256, 256)].T

    @pl.when(xc >= 2)
    def _():
        for r in range(4):
            wt[r // 2, pl.ds(r % 2 * 256, 256), :] = ru[:, pl.ds(r * 256, 256)].T

    def w_rows(at):
        return pl.ds(pl.multiple_of(at * KW + (xc % 2) * 16, 16), 16)

    def send_w(j):
        at = (ring + 1 + j) % 16
        pltpu.make_async_remote_copy(
            src_ref=wt.at[:, w_rows(at)], dst_ref=wp.at[xc, ring], send_sem=w_send.at[0], recv_sem=w_recv.at[0],
            device_id=(dp, yh * 16 + at), device_id_type=MESH,
        ).start()

    pl.semaphore_wait(barrier, NBLK - 1 + 3 + 1 + 4 - stays)
    tiles(15, send_w)
    loads["x0"].wait()
    z_event(0, 0)
    loads["x1"].wait()
    z_event(1, 0)
    wp[xc, ring] = wt[:, w_rows(ring), :]

    loads["dy"].wait()
    loads["ld"].wait()

    def back_down(q):
        rows = rows_at(q, 256)
        for h in range(2):
            toks = dy[h * HALF:(h + 1) * HALF, :]
            dsend[h, rows, :] = dot(ld[pl.ds(pl.multiple_of((1 - yh) * 512 + q * 256, 256), 256), :], toks, NT).astype(BF)
            dd[yh, h, rows, :] = dot(ld[pl.ds(pl.multiple_of(yh * 512 + q * 256, 256), 256), :], toks, NT).astype(BF)

    tiles(2, back_down)
    to_y = pltpu.make_async_remote_copy(
        src_ref=dsend, dst_ref=dd.at[yh], send_sem=d_send.at[0], recv_sem=d_recv.at[0],
        device_id=(dp, over_y), device_id_type=MESH,
    )
    to_y.start()

    HOPS = (8, 7, 9, 6, 10, 5, 11, 12, 4, 13, 3, 14, 2, 15, 1)

    def relay(held, dst, send_sem, recv_sem, start=0, end=15, h=slice(None)):
        for hop in HOPS[start:end]:
            at = (ring + hop) % 16
            pltpu.make_async_remote_copy(
                src_ref=held.at[:, h, rows_at(at, KW)], dst_ref=dst.at[:, h, rows_at(ring, KW)],
                send_sem=send_sem, recv_sem=recv_sem, device_id=(dp, yh * 16 + at), device_id_type=MESH,
            ).start()
        if end == 15:
            dst[:, h, rows_at(ring, KW), :] = held[:, h, rows_at(ring, KW), :]

    def flip_blocks(src, dst):
        def body(i):
            r, c = i // 4, i % 4
            dst[c * 4 + r] = src[rows_at(r, 256), rows_at(c, 256)].T

        tiles(16, body)

    def block_row(t, q):
        return jnp.concatenate([t[q * 4 + c] for c in range(4)], axis=1)

    loads["lg"].wait()
    flip_blocks(lg, lgt)

    await_bytes(wp.at[0, pl.ds(0, 15)], w_recv.at[0])

    def share_w(j):
        to = ((xc + 1 + j) % 4) * 2 + yl
        pltpu.make_async_remote_copy(
            src_ref=wp.at[xc], dst_ref=wp.at[xc], send_sem=w_send.at[1], recv_sem=w_recv.at[1],
            device_id=(to, tn), device_id_type=MESH,
        ).start()

    tiles(3, share_w)

    def columns(b, *ys):
        return jnp.concatenate([wp[p, b, y] for y in ys for p in range(4)], axis=0)

    def first(h, *ks):
        for k in ks:
            await_bytes(xall.at[h, 0], c_recv.at[h, k])
            at = (z + OFFS[h][k]) % 8

            def body(c, at=at):
                b = at * 2 + c
                w = columns(b, yh, 1 - yh)
                v = dot(w, xall[h, b], NT).astype(BF)
                own, rows = rows_at(yh * 16 + b, KW), rows_at(b, KW)
                gum[h, 0, own, :] = v[0:32]
                gum[h, 1, own, :] = v[32:64]
                ps[h, 0, rows, :] = v[64:96]
                ps[h, 1, rows, :] = v[96:128]
                pltpu.make_async_remote_copy(
                    src_ref=ps.at[h, :, rows], dst_ref=gum.at[h, :, own], send_sem=p_send.at[h], recv_sem=p_recv.at[h],
                    device_id=(dp, over_y), device_id_type=MESH,
                ).start()

            tiles(2, body)

    def events(h, *ks):
        for k in ks:
            z_event(h, k)

    loads["lu"].wait()
    flip_blocks(lu, lut)
    events(0, 1, 2)
    events(1, 1, 2)
    loads["rd"].wait()
    for r in range(4):
        flip(rd, rdt, 4, r)
    events(0, 3, 4)
    events(1, 3, 4)
    for r in range(4):
        flip(ld, ldt, 1, r)
    await_bytes(wp.at[pl.ds(0, 3)], w_recv.at[1])
    first(0, 0, 1, 2, 3, 4)
    events(0, 5, 6)
    events(1, 5, 6)
    to_y.wait_recv()
    relay(dd, rdd, d_send.at[1], d_recv.at[1], 0, 4)
    first(0, 5, 6)
    first(1, 0, 1, 2)
    events(0, 7)
    events(1, 7)
    relay(dd, rdd, d_send.at[1], d_recv.at[1], 4, 15)
    first(0, 7)
    first(1, 3, 4, 5, 6, 7)

    downs = []

    def forward(h):
        await_bytes(gum.at[h, :, pl.ds(0, 512)], p_recv.at[h])

        def body(q):
            rows = rows_at(q, 256)
            g = dot(block_row(lgt, q), gum[h, 0])
            u = dot(block_row(lut, q), gum[h, 1])
            gate[h, rows, :] = g
            upper[h, rows, :] = u
            hidden[h, rows, :] = (g * jax.nn.sigmoid(g) * u).astype(BF)

        unrolled(4, body)

        def down_over(q):
            rows = pl.ds(pl.multiple_of((1 - yh) * 512 + q * 256, 256), 256)
            msend[h, rows_at(q, 256), :] = dot(rdt[rows, :], hidden[h]).astype(BF)

        unrolled(2, down_over)
        cp = pltpu.make_async_remote_copy(
            src_ref=msend.at[h], dst_ref=dm.at[yh, h], send_sem=m_send.at[h], recv_sem=m_recv.at[h],
            device_id=(dp, over_y), device_id_type=MESH,
        )
        cp.start()
        downs.append(cp)

        def down_here(q):
            rows = pl.ds(pl.multiple_of(yh * 512 + q * 256, 256), 256)
            dm[yh, h, rows_at(q, 256), :] = dot(rdt[rows, :], hidden[h]).astype(BF)

        unrolled(2, down_here)

    forward(0)
    forward(1)
    await_bytes(rdd.at[:, :, pl.ds(0, 480)], d_recv.at[1])

    def backward(h):
        def body(q):
            rows = rows_at(q, 256)
            dh = dot(rd[rows, 0:512], rdd[0, h]) + dot(rd[rows, 512:1024], rdd[1, h])
            g, u = gate[h, rows, :], upper[h, rows, :]
            s = jax.nn.sigmoid(g)
            dgate[h, rows, :] = (dh * u * s * (1.0 + g * (1.0 - s))).astype(BF)
            dup[h, rows, :] = (dh * (g * s)).astype(BF)

        unrolled(4, body)

    nxt, prv, opp = (xc + 1) % 4, (xc + 3) % 4, (xc + 2) % 4

    def ship(src, dst, sem, to):
        cp = pltpu.make_async_remote_copy(
            src_ref=src, dst_ref=dst, send_sem=ring_send.at[sem], recv_sem=ring_recv.at[sem],
            device_id=to, device_id_type=MESH,
        )
        cp.start()
        return cp

    to_next, to_prev = (nxt * 2 + yl, tn), (prv * 2 + yl, tn)
    to_pair = (xc * 2 + 1 - yl, tn)
    big = (
        (hidden, rdd, rd_v, rd_o),
        (gum.at[:, 0], dgate, lg_v, lg_o),
        (gum.at[:, 1], dup, lu_v, lu_o),
    )

    def part(a, q, half):
        if a == 3:
            return part_in(summed_block(2 * q + yl, half)) + wyin[q, half].astype(F32)
        if a == 4:
            rows = pl.ds(pl.multiple_of(q % 2 * 256 + half * 128, 128), 128)
            return dot(rdm[q // 2, 0, rows, :], dy[0:HALF, :]) + dot(rdm[q // 2, 1, rows, :], dy[HALF:, :])
        rows = pl.ds(pl.multiple_of(q * 256 + half * 128, 128), 128)
        if a in (2, 5):
            cols = slice(0, 512) if a == 2 else slice(512, 1024)
            return dot(gum[0, 1, rows, :], dup[0, cols, :], NT) + dot(gum[1, 1, rows, :], dup[1, cols, :], NT)
        left, right = big[a][:2]

        def both(pick):
            return dot(left[0, rows, :], pick(0), NT) + dot(left[1, rows, :], pick(1), NT)

        if a == 0:
            return jnp.concatenate([both(lambda h, y=y: rdd[y, h]) for y in range(2)], axis=1)
        return both(lambda h: right[h])

    started = [[None] * 5 for _ in range(6)]
    steps = (p2, pn, pp, ysend, ra, rb, rc, rdn, ye)
    places = [tuple(ref.at[a] for ref in steps) for a in range(2)]

    def columns_of(a):
        at = pl.ds(0 if a == 2 else 512, 512)
        return tuple(ref.at[2, :, :, at] if ref.ndim == 4 else ref.at[2, :, at] for ref in steps)

    places.append(columns_of(2))
    for ref in (wring, lring):
        places.append(tuple(
            ref.at[at] if size == 1 else ref.at[pl.ds(at, size)]
            for at, size in ((0, 2), (2, 2), (4, 2), (6, 1), (7, 1), (8, 1), (9, 2), (11, 2), (13, 1))
        ))
    places.append(columns_of(5))

    crossed = []

    def cross_first():
        for n, q in enumerate((opp, nxt, prv, xc)):
            for half in range(2):
                wyout[q, half] = part_in(summed_block(2 * q + 1 - yl, half)).astype(BF)
            cp = pltpu.make_async_remote_copy(
                src_ref=wyout.at[q], dst_ref=wyin.at[q], send_sem=cross_send.at[n], recv_sem=cross_recv.at[n],
                device_id=to_pair, device_id_type=MESH,
            )
            cp.start()
            crossed.append(cp)

    def ring1(a):
        p2, _, _, _, ra, rb = places[a][:6]
        if a == 3:
            crossed[0].wait_recv()

        def put(half):
            p2[half] = part(a, opp, half).astype(BF)

        tiles(2, put)
        started[a][0] = ship(p2.at[0], ra, 5 * a, to_next)
        started[a][1] = ship(p2.at[1], rb, 5 * a + 1, to_prev)

    def ring2(a):
        _, pn, pp, _, ra, rb, rc, rdn, _ = places[a]
        if a == 3:
            crossed[1].wait_recv()
            crossed[2].wait_recv()

        def put_n(half):
            pn[half] = part(a, nxt, half).astype(BF)

        def put_p(half):
            pp[half] = part(a, prv, half).astype(BF)

        tiles(2, put_n)
        started[a][0].wait_recv()
        pn[0] = (pn[0].astype(F32) + ra[...].astype(F32)).astype(BF)
        started[a][2] = ship(pn, rc, 5 * a + 2, to_next)
        tiles(2, put_p)
        started[a][1].wait_recv()
        pp[1] = (pp[1].astype(F32) + rb[...].astype(F32)).astype(BF)
        started[a][3] = ship(pp, rdn, 5 * a + 3, to_prev)

    def kept(a, c):
        return c % 2, pl.ds((a * 2 + c // 2) * 128, 128)

    def ring3(a):
        _, _, _, ysend, _, _, rc, rdn, ye = places[a]
        if a == 3:
            crossed[3].wait_recv()
        started[a][2].wait_recv()
        started[a][3].wait_recv()

        def total(half):
            return part(a, xc, half) + rc[half].astype(F32) + rdn[half].astype(F32)

        if a == 3:
            for half in range(2):
                wsum[half * 128:(half + 1) * 128, :] = total(half).astype(BF)
            return
        ysend[...] = total(1 - yl).astype(BF)
        started[a][4] = ship(ysend, ye, 5 * a + 4, to_pair)
        own = total(yl)
        if a == 4:
            lown[...] = own
            return
        for c, cols in wide_columns(a):
            s, rows = kept(min(a, 2), c)
            upper[s, rows, :] = own[:, cols]

    def wide_columns(a):
        first = 2 if a == 5 else 0
        return [(first + c, slice(c * 256, (c + 1) * 256)) for c in range(2 if a in (2, 5) else 4)]

    def ring4(a):
        ye = places[a][8]
        started[a][4].wait_recv()
        if a == 4:
            ld_v[...] = (lown[...] + ye[...].astype(F32)).astype(BF)
            store(ld_v, ld_o.at[0])
            return
        out, out_h = big[min(a, 2)][2:]
        for c, cols in wide_columns(a):
            s, rows = kept(min(a, 2), c)
            out[:, c * 256:(c + 1) * 256] = (upper[s, rows, :] + ye[:, cols].astype(F32)).astype(BF)
        if a != 2:
            store(out, out_h.at[0])

    for h in range(2):
        await_bytes(ps.at[h], p_send.at[h])
    crossing = []

    def mids_over(gu, h):
        w, d = ((lg, dgate), (lu, dup))[gu]
        for q in range(2):
            src = pl.ds(pl.multiple_of((1 - yh) * 512 + q * 256, 256), 256)
            ps[gu, h, q * 256:(q + 1) * 256, :] = dot(w[src, :], d[h]).astype(BF)
        cp = pltpu.make_async_remote_copy(
            src_ref=ps.at[gu, h], dst_ref=back.at[yh, gu, h], send_sem=b_send.at[gu * 2 + h], recv_sem=b_recv.at[gu * 2 + h],
            device_id=(dp, over_y), device_id_type=MESH,
        )
        cp.start()
        crossing.append(cp)

    def mids_here(gu, h):
        w, d = ((lg, dgate), (lu, dup))[gu]
        for q in range(2):
            src = pl.ds(pl.multiple_of(yh * 512 + q * 256, 256), 256)
            back[yh, gu, h, q * 256:(q + 1) * 256, :] = dot(w[src, :], d[h]).astype(BF)

    ring1(0)
    backward(0)
    mids_over(0, 0)
    mids_over(1, 0)
    downs[0].wait_recv()
    relay(dm, rdm, m_send.at[2], m_recv.at[2], 0, 15, 0)
    backward(1)
    mids_over(0, 1)
    mids_over(1, 1)
    ring1(1)
    downs[1].wait_recv()
    relay(dm, rdm, m_send.at[3], m_recv.at[3], 0, 7, 1)
    ring1(2)
    ring1(5)
    mids_here(0, 0)
    mids_here(1, 0)
    ring2(0)
    mids_here(0, 1)
    mids_here(1, 1)
    ring2(1)

    def outputs():
        for h in range(2):
            await_bytes(rdm.at[:, h, pl.ds(0, 480)], m_recv.at[2 + h])
        ring1(4)
        for h in range(2):
            out_v[h * HALF:(h + 1) * HALF, :] = (
                dot(ldt[:, 0:512], rdm[0, h]) + dot(ldt[:, 512:], rdm[1, h])
            ).T.astype(BF)
        store(out_v, out_o)

    def stacked(h, b):
        rows = rows_at(b, KW)
        return jnp.concatenate([back[y, gu, h, rows, :] for y in range(2) for gu in range(2)], axis=0)

    def dx_part(h, zz, c):
        b = zz * 2 + c
        return dot(stacked(h, b), columns(b, 0, 1), TN)

    def for_sibling(h):
        for cp in crossing[2 * h:2 * h + 2]:
            cp.wait_recv()
        for d in range(8):
            zz = (z + 4 + d) % 8
            lgt[h * 8 + zz] = dx_part(h, zz, 1 - core).astype(BF)
            pltpu.make_async_remote_copy(
                src_ref=lgt.at[h * 8 + zz], dst_ref=sums_in.at[h, zz], send_sem=s_send.at[0], recv_sem=s_recv.at[h, d],
                device_id=(dp, sibling), device_id_type=MESH,
            ).start()

    def slab_sum(h, off):
        zz = (z + off) % 8
        await_bytes(sums_in.at[h, zz], s_recv.at[h, (off + 4) % 8])
        return dx_part(h, zz, core) + sums_in[h, zz].astype(F32)

    REACH = ((4, 3), (3, 4))
    links = []

    def chain(d, h):
        for way, (sign, to) in enumerate(((1, up_z), (-1, down_z))):
            far = REACH[h][way]
            if d > far:
                continue
            v = slab_sum(h, sign * d)
            if d < far:
                await_bytes(chain_in.at[h, way, d], ch_recv.at[h, way, d])
                v = v + chain_in[h, way, d].astype(F32)
            slot = (h * 2 + way) * 4 + d - 1
            lut[slot] = v.astype(BF)
            cp = pltpu.make_async_remote_copy(
                src_ref=lut.at[slot], dst_ref=chain_in.at[h, way, d - 1],
                send_sem=ch_send.at[slot], recv_sem=ch_recv.at[h, way, d - 1],
                device_id=(dp, to), device_id_type=MESH,
            )
            cp.start()
            links.append(cp)

    def part_in(b):
        return dot(stacked(0, b), xall[0, b]) + dot(stacked(1, b), xall[1, b])

    def tokens_grad(h):
        v = slab_sum(h, 0)
        for way in range(2):
            await_bytes(chain_in.at[h, way, 0], ch_recv.at[h, way, 0])
            v = v + chain_in[h, way, 0].astype(F32)
        dx_v[h * HALF:(h + 1) * HALF, :] = v.astype(BF)

    for_sibling(0)
    chain(4, 0)
    chain(3, 0)
    for_sibling(1)
    chain(4, 1)
    cross_first()
    chain(2, 0)
    relay(dm, rdm, m_send.at[3], m_recv.at[3], 7, 15, 1)
    ring1(3)
    ring2(2)
    ring3(0)
    chain(3, 1)
    ring2(3)
    outputs()
    ring2(5)
    chain(1, 0)
    ring3(1)
    chain(2, 1)

    ring3(3)
    final = []
    for par in range(2):
        for cs in range(2):
            to = (cs * 4 + ring // 4, yh * 16 + summed_block(dp, par))
            src, dst = wsum.at[pl.ds(par * 128 + cs * 64, 64)], wfin.at[ring % 4]
            away = pltpu.make_async_remote_copy(
                src_ref=src, dst_ref=dst, send_sem=wf_send.at[par * 2 + cs], recv_sem=wf_recv.at[0],
                device_id=to, device_id_type=MESH,
            )

            def keep(src=src, dst=dst):
                pltpu.make_async_copy(src, dst, wf_recv.at[0]).start()

            apart(*to, keep, away.start)
            final.append((to, away))
    ring3(2)
    ring2(4)
    tokens_grad(0)
    chain(1, 1)
    ring4(0)
    ring3(5)
    ring3(4)
    ring4(1)
    tokens_grad(1)
    store(dx_v, dx_o)
    ring4(2)
    ring4(5)
    await_bytes(wfin, wf_recv.at[0])
    for gu, (out, out_h) in enumerate(((rg_v, rg_o), (ru_v, ru_o))):
        out[...] = jnp.concatenate([wfin[j, gu * KW:(gu + 1) * KW, :] for j in range(4)], axis=0).T
        store(out, out_h.at[0])
    ring4(4)

    for h in range(2):
        await_bytes(xall.at[h, pl.ds(0, 15)], x_send.at[h])
    to_y.wait_send()
    await_bytes(rdd.at[:, :, pl.ds(0, 480)], d_send.at[1])
    await_bytes(wp.at[0, pl.ds(0, 15)], w_send.at[0])
    await_bytes(wp.at[pl.ds(0, 3)], w_send.at[1])
    for h in range(2):
        await_bytes(rdm.at[:, h, pl.ds(0, 480)], m_send.at[2 + h])
    for cp in crossing + links + downs:
        cp.wait_send()
    await_bytes(sums_in, s_send.at[0])
    for group in started + [crossed]:
        for cp in group:
            if cp is not None:
                cp.wait_send()
    for to, away in final:
        apart(*to, lambda: None, away.wait_send)
    for cp in stores:
        cp.wait()


def hand_over(*refs):
    src, dst, held, (sem,) = refs[:8], refs[8:16], refs[16:24], refs[24:]
    arriving = [pltpu.make_async_copy(src[i], held[i], sem.at[0, i]) for i in range(8)]
    leaving = [pltpu.make_async_copy(held[i], dst[i], sem.at[1, i]) for i in range(8)]
    for cp in arriving:
        cp.start()
    for i in range(8):
        arriving[i].wait()
        leaving[i].start()
    for cp in leaving:
        cp.wait()


def per_device(tokens, gate_in, gate_out, up_in, up_out, down_in, down_out, cotangent):
    anyw = pl.BlockSpec(memory_space=pl.ANY)
    out_shape = (
        jax.ShapeDtypeStruct((TOK, DB), BF),
        jax.ShapeDtypeStruct((TOK, DB), BF),
        jax.ShapeDtypeStruct((1, DB, 128), BF),
        jax.ShapeDtypeStruct((1, 128, MB), BF),
        jax.ShapeDtypeStruct((1, DB, 128), BF),
        jax.ShapeDtypeStruct((1, 128, MB), BF),
        jax.ShapeDtypeStruct((1, 128, MB), BF),
        jax.ShapeDtypeStruct((1, 128, DB), BF),
    )
    V = pltpu.VMEM
    mids = V((2, MB, HALF), BF)
    wide = V((2, MB, HALF), F32)
    square = V((MB, MB), BF)
    dma = pltpu.SemaphoreType.DMA
    scratch = [
        V((TOK, DB), BF), V((TOK, DB), BF), V((DB, 128), BF), V((128, MB), BF),
        V((DB, 128), BF), V((128, MB), BF), V((128, MB), BF), V((128, DB), BF),
        V((2, 16, HALF, DB), BF), V((2, 512, DB), BF), V((4, 16, 2, 16, DB), BF), V((2, 2, 512, HALF), BF),
        V((DB, MB), BF), square, V((DB, MB), BF), square, square, V((MB, DB), BF), V((TOK, DB), BF),
        V((16, 256, 256), BF), V((16, 256, 256), BF), square, V((DB, MB), BF),
        V((2, 512, HALF), BF), V((2, 2, 512, HALF), BF), V((2, 2, 512, HALF), BF),
        V((2, 512, HALF), BF), V((2, 2, 512, HALF), BF), V((2, 2, 512, HALF), BF), V((2, 2, MB, HALF), BF),
        V((2, 2, 2, 512, HALF), BF), V((2, 8, HALF, DB), BF), V((2, 2, 4, HALF, DB), BF),
        wide, wide, mids, mids, mids,
        V((3, 2, 128, MB), BF), V((3, 2, 128, MB), BF), V((3, 2, 128, MB), BF), V((3, 128, MB), BF),
        V((3, 128, MB), BF), V((3, 128, MB), BF), V((3, 2, 128, MB), BF), V((3, 2, 128, MB), BF), V((3, 128, MB), BF),
        V((14, 128, DB), BF), V((14, 128, DB), BF), V((4, 2, 128, DB), BF), V((4, 2, 128, DB), BF),
        V((128, DB), F32), V((256, DB), BF), V((4, 64, DB), BF),
        dma((9,)), dma((8,)), dma((2,)), dma((2, 8)), dma((2, 8)), dma((2,)), dma((2,)), dma((2,)), dma((2,)),
        dma((2,)), dma((2,)),
        dma((4,)), dma((4,)), dma((30,)), dma((30,)), dma((4,)), dma((4,)),
        dma((4,)), dma((4,)), dma((1,)), dma((2, 8)), dma((16,)), dma((2, 2, 4)), dma((4,)), dma((1,)),
    ]
    results = pl.pallas_call(
        kernel,
        out_shape=out_shape,
        in_specs=[anyw] * 8,
        out_specs=(anyw,) * 8,
        scratch_shapes=scratch,
        compiler_params=pltpu.CompilerParams(
            collective_id=0, has_side_effects=True, vmem_limit_bytes=62 * 2**20
        ),
        cost_estimate=pl.CostEstimate(flops=12_000_000_000, bytes_accessed=10_000_000, transcendentals=1_000_000),
    )(tokens, gate_in, gate_out, up_in, up_out, down_in, down_out, cotangent)
    return pl.pallas_call(
        hand_over,
        out_shape=out_shape,
        in_specs=[anyw] * 8,
        out_specs=(anyw,) * 8,
        scratch_shapes=[V(o.shape, BF) for o in out_shape] + [pltpu.SemaphoreType.DMA((2, 8))],
    )(*results)


def solution(mesh):
    in_specs = (
        P("dp", "tensor"),
        P("tensor", None, None),
        P("tensor", None, None),
        P("tensor", None, None),
        P("tensor", None, None),
        P("tensor", None, None),
        P("tensor", None, None),
        P("dp", "tensor"),
    )
    out_specs = (
        P("dp", "tensor"),
        P("dp", "tensor"),
        P("tensor", None, "dp"),
        P("tensor", "dp", None),
        P("tensor", None, "dp"),
        P("tensor", "dp", None),
        P("tensor", "dp", None),
        P("tensor", "dp", None),
    )
    return jax.shard_map(
        per_device, mesh=mesh, in_specs=in_specs, out_specs=out_specs, check_vma=False
    )
```

```python
import jax
import jax.numpy as jnp
from jax import lax
from jax.experimental import pallas as pl
from jax.experimental.pallas import tpu as pltpu
from jax.sharding import PartitionSpec as P

MESH = pl.DeviceIdType.MESH
BF = jnp.bfloat16
F32 = jnp.float32
NT = (((1,), (1,)), ((), ()))
NN = (((1,), (0,)), ((), ()))
TN = (((0,), (0,)), ((), ()))
TOK, HALF, DB, MB, KW, NBLK, NDP = 512, 256, 256, 1024, 32, 32, 8


def dot(a, b, form=NN):
    return lax.dot_general(a, b, form, preferred_element_type=F32)


def rows_at(index, size):
    start = index * size
    return pl.ds(start if isinstance(start, int) else pl.multiple_of(start, size), size)


def tiles(count, body):
    def step(i, carry):
        body(i)
        return carry

    lax.fori_loop(0, count, step, 0)


def unrolled(count, body):
    for i in range(count):
        body(i)


def kernel(
    x_h, rg_h, lg_h, ru_h, lu_h, rd_h, ld_h, dy_h,
    out_o, dx_o, rg_o, lg_o, ru_o, lu_o, rd_o, ld_o,
    out_v, dx_v, rg_v, lg_v, ru_v, lu_v, rd_v, ld_v,
    xall, wt, wp, ps, rg, lg, ru, lu, rd, ld, dy,
    lgt, lut, rdt, ldt,
    dsend, dd, rdd, msend, dm, rdm, gum, back, sums_in, chain_in,
    gate, upper, hidden, dgate, dup,
    p2, pn, pp, ysend, ra, rb, rc, rdn, ye,
    wring, lring, wyout, wyin, lown, wsum, wfin,
    load_sem, store_sem, x_send, z_recv, c_recv, p_send, p_recv, d_send, d_recv, w_send, w_recv,
    m_send, m_recv, ring_send, ring_recv, cross_send, cross_recv,
    b_send, b_recv, s_send, s_recv, ch_send, ch_recv, wf_send, wf_recv,
):
    dp, tn = lax.axis_index("dp"), lax.axis_index("tensor")
    xc, yl = dp // 2, dp % 2
    yh, z, core = tn // 16, (tn // 2) % 8, tn % 2

    def block(y, zz, c):
        return (y * 8 + zz) * 2 + c

    def await_bytes(ref, sem):
        pltpu.make_async_copy(ref, ref, sem).wait()

    ring = z * 2 + core
    loads = {}
    for i, (name, src, dst) in enumerate((
        ("rg", rg_h.at[0], rg), ("ru", ru_h.at[0], ru),
        ("x0", x_h.at[pl.ds(0, HALF)], xall.at[0, ring]), ("x1", x_h.at[pl.ds(HALF, HALF)], xall.at[1, ring]),
        ("ld", ld_h.at[0], ld), ("dy", dy_h, dy), ("lg", lg_h.at[0], lg), ("lu", lu_h.at[0], lu), ("rd", rd_h.at[0], rd),
    )):
        loads[name] = pltpu.make_async_copy(src, dst, load_sem.at[i])
        loads[name].start()

    stores = []

    def store(src, dst):
        cp = pltpu.make_async_copy(src, dst, store_sem.at[len(stores)])
        cp.start()
        stores.append(cp)

    def peer(j):
        g = j // 4
        dz = 4 + (1 - 2 * (g % 2)) * ((g + 1) // 2)
        return block((yh + 1 - (j // 2) % 2) % 2, (z + dz) % 8, (core + 1 - j % 2) % 2)

    def dp_peer(j):
        return (dp + 2 * j + 2) % NDP

    barrier = pltpu.get_barrier_semaphore()

    def greet_tensor(j):
        pl.semaphore_signal(barrier, inc=1, device_id=(dp, peer(j)), device_id_type=MESH)

    def greet_dp(j):
        pl.semaphore_signal(barrier, inc=1, device_id=(dp_peer(j), tn), device_id_type=MESH)

    tiles(NBLK - 1, greet_tensor)
    tiles(3, greet_dp)
    pl.semaphore_signal(barrier, inc=1, device_id=(xc * 2 + 1 - yl, tn), device_id_type=MESH)

    def apart(to_dp, to_tn, here, there):
        same = jnp.logical_and(to_dp == dp, to_tn == tn)
        pl.when(same)(here)
        pl.when(jnp.logical_not(same))(there)

    def summed_block(d, par):
        return ((z + d + par * (8 - 2 * d)) % 8) * 2 + par

    for j in range(4):
        away = 8 + z - (2 * (dp % 4) + j // 2)
        source = ((away * (1 + 6 * core)) % 8, yh * 16 + 4 * (dp % 4) + j)

        def greet_source(source=source):
            pl.semaphore_signal(barrier, inc=1, device_id=source, device_id_type=MESH)

        apart(*source, lambda: None, greet_source)
    stays = jnp.logical_and(dp == 0, z < 2).astype(jnp.int32)

    OFFS = ((0, -1, 1, -2, 2, -3, 3, -4), (0, -1, 1, -2, 2, -3, 3, 4))

    def x_copy(h, b, sem, to):
        pltpu.make_async_remote_copy(
            src_ref=xall.at[h, b], dst_ref=xall.at[h, b], send_sem=x_send.at[h], recv_sem=sem,
            device_id=(dp, to), device_id_type=MESH,
        ).start()

    up_z, down_z = block(yh, (z + 1) % 8, core), block(yh, (z + 7) % 8, core)
    over_y, sibling = block(1 - yh, z, core), block(yh, z, 1 - core)

    def z_event(h, k):
        off = OFFS[h][k]
        b = ((z + off) % 8) * 2 + core
        if k:
            await_bytes(xall.at[h, b], z_recv.at[h, k])
        for sign, to in ((-1, up_z), (1, down_z)):
            if (off == 0 or off * sign > 0) and off + sign in OFFS[h]:
                x_copy(h, b, z_recv.at[h, OFFS[h].index(off + sign)], to)
        x_copy(h, b, c_recv.at[h, k], sibling)

    def flip(src, dst, across, r):
        def body(c):
            dst[rows_at(c, 256), pl.ds(r * 256, 256)] = src[pl.ds(r * 256, 256), rows_at(c, 256)].T

        tiles(across, body)

    loads["rg"].wait()
    loads["ru"].wait()

    @pl.when(xc < 2)
    def _():
        for r in range(4):
            wt[r // 2, pl.ds(r % 2 * 256, 256), :] = rg[:, pl.ds(r * 256, 256)].T

    @pl.when(xc >= 2)
    def _():
        for r in range(4):
            wt[r // 2, pl.ds(r % 2 * 256, 256), :] = ru[:, pl.ds(r * 256, 256)].T

    def w_rows(at):
        return pl.ds(pl.multiple_of(at * KW + (xc % 2) * 16, 16), 16)

    def send_w(j):
        at = (ring + 1 + j) % 16
        pltpu.make_async_remote_copy(
            src_ref=wt.at[:, w_rows(at)], dst_ref=wp.at[xc, ring], send_sem=w_send.at[0], recv_sem=w_recv.at[0],
            device_id=(dp, yh * 16 + at), device_id_type=MESH,
        ).start()

    pl.semaphore_wait(barrier, NBLK - 1 + 3 + 1 + 4 - stays)
    tiles(15, send_w)
    loads["x0"].wait()
    z_event(0, 0)
    loads["x1"].wait()
    z_event(1, 0)
    wp[xc, ring] = wt[:, w_rows(ring), :]

    loads["dy"].wait()
    loads["ld"].wait()

    def back_down(q):
        rows = rows_at(q, 256)
        for h in range(2):
            toks = dy[h * HALF:(h + 1) * HALF, :]
            dsend[h, rows, :] = dot(ld[pl.ds(pl.multiple_of((1 - yh) * 512 + q * 256, 256), 256), :], toks, NT).astype(BF)
            dd[yh, h, rows, :] = dot(ld[pl.ds(pl.multiple_of(yh * 512 + q * 256, 256), 256), :], toks, NT).astype(BF)

    tiles(2, back_down)
    to_y = pltpu.make_async_remote_copy(
        src_ref=dsend, dst_ref=dd.at[yh], send_sem=d_send.at[0], recv_sem=d_recv.at[0],
        device_id=(dp, over_y), device_id_type=MESH,
    )
    to_y.start()

    HOPS = (8, 7, 9, 6, 10, 5, 11, 12, 4, 13, 3, 14, 2, 15, 1)

    def relay(held, dst, send_sem, recv_sem, start=0, end=15, h=slice(None)):
        for hop in HOPS[start:end]:
            at = (ring + hop) % 16
            pltpu.make_async_remote_copy(
                src_ref=held.at[:, h, rows_at(at, KW)], dst_ref=dst.at[:, h, rows_at(ring, KW)],
                send_sem=send_sem, recv_sem=recv_sem, device_id=(dp, yh * 16 + at), device_id_type=MESH,
            ).start()
        if end == 15:
            dst[:, h, rows_at(ring, KW), :] = held[:, h, rows_at(ring, KW), :]

    def flip_blocks(src, dst):
        def body(i):
            r, c = i // 4, i % 4
            dst[c * 4 + r] = src[rows_at(r, 256), rows_at(c, 256)].T

        tiles(16, body)

    def block_row(t, q):
        return jnp.concatenate([t[q * 4 + c] for c in range(4)], axis=1)

    loads["lg"].wait()
    flip_blocks(lg, lgt)

    await_bytes(wp.at[0, pl.ds(0, 15)], w_recv.at[0])

    def share_w(j):
        to = ((xc + 1 + j) % 4) * 2 + yl
        pltpu.make_async_remote_copy(
            src_ref=wp.at[xc], dst_ref=wp.at[xc], send_sem=w_send.at[1], recv_sem=w_recv.at[1],
            device_id=(to, tn), device_id_type=MESH,
        ).start()

    tiles(3, share_w)

    def columns(b, *ys):
        return jnp.concatenate([wp[p, b, y] for y in ys for p in range(4)], axis=0)

    def first(h, *ks):
        for k in ks:
            await_bytes(xall.at[h, 0], c_recv.at[h, k])
            at = (z + OFFS[h][k]) % 8

            def body(c, at=at):
                b = at * 2 + c
                w = columns(b, yh, 1 - yh)
                v = dot(w, xall[h, b], NT).astype(BF)
                own, rows = rows_at(yh * 16 + b, KW), rows_at(b, KW)
                gum[h, 0, own, :] = v[0:32]
                gum[h, 1, own, :] = v[32:64]
                ps[h, 0, rows, :] = v[64:96]
                ps[h, 1, rows, :] = v[96:128]
                pltpu.make_async_remote_copy(
                    src_ref=ps.at[h, :, rows], dst_ref=gum.at[h, :, own], send_sem=p_send.at[h], recv_sem=p_recv.at[h],
                    device_id=(dp, over_y), device_id_type=MESH,
                ).start()

            tiles(2, body)

    def events(h, *ks):
        for k in ks:
            z_event(h, k)

    loads["lu"].wait()
    flip_blocks(lu, lut)
    events(0, 1, 2)
    events(1, 1, 2)
    loads["rd"].wait()
    for r in range(4):
        flip(rd, rdt, 4, r)
    events(0, 3, 4)
    events(1, 3, 4)
    for r in range(4):
        flip(ld, ldt, 1, r)
    await_bytes(wp.at[pl.ds(0, 3)], w_recv.at[1])
    first(0, 0, 1, 2, 3, 4)
    events(0, 5, 6)
    events(1, 5, 6)
    to_y.wait_recv()
    relay(dd, rdd, d_send.at[1], d_recv.at[1], 0, 4)
    first(0, 5, 6)
    first(1, 0, 1, 2)
    events(0, 7)
    events(1, 7)
    relay(dd, rdd, d_send.at[1], d_recv.at[1], 4, 15)
    first(0, 7)
    first(1, 3, 4, 5, 6, 7)

    downs = []

    def forward(h):
        await_bytes(gum.at[h, :, pl.ds(0, 512)], p_recv.at[h])

        def body(q):
            rows = rows_at(q, 256)
            g = dot(block_row(lgt, q), gum[h, 0])
            u = dot(block_row(lut, q), gum[h, 1])
            gate[h, rows, :] = g
            upper[h, rows, :] = u
            hidden[h, rows, :] = (g * jax.nn.sigmoid(g) * u).astype(BF)

        unrolled(4, body)

        def down_over(q):
            rows = pl.ds(pl.multiple_of((1 - yh) * 512 + q * 256, 256), 256)
            msend[h, rows_at(q, 256), :] = dot(rdt[rows, :], hidden[h]).astype(BF)

        unrolled(2, down_over)
        cp = pltpu.make_async_remote_copy(
            src_ref=msend.at[h], dst_ref=dm.at[yh, h], send_sem=m_send.at[h], recv_sem=m_recv.at[h],
            device_id=(dp, over_y), device_id_type=MESH,
        )
        cp.start()
        downs.append(cp)

        def down_here(q):
            rows = pl.ds(pl.multiple_of(yh * 512 + q * 256, 256), 256)
            dm[yh, h, rows_at(q, 256), :] = dot(rdt[rows, :], hidden[h]).astype(BF)

        unrolled(2, down_here)

    forward(0)
    forward(1)
    await_bytes(rdd.at[:, :, pl.ds(0, 480)], d_recv.at[1])

    def backward(h):
        def body(q):
            rows = rows_at(q, 256)
            dh = dot(rd[rows, 0:512], rdd[0, h]) + dot(rd[rows, 512:1024], rdd[1, h])
            g, u = gate[h, rows, :], upper[h, rows, :]
            s = jax.nn.sigmoid(g)
            dgate[h, rows, :] = (dh * u * s * (1.0 + g * (1.0 - s))).astype(BF)
            dup[h, rows, :] = (dh * (g * s)).astype(BF)

        unrolled(4, body)

    nxt, prv, opp = (xc + 1) % 4, (xc + 3) % 4, (xc + 2) % 4

    def ship(src, dst, sem, to):
        cp = pltpu.make_async_remote_copy(
            src_ref=src, dst_ref=dst, send_sem=ring_send.at[sem], recv_sem=ring_recv.at[sem],
            device_id=to, device_id_type=MESH,
        )
        cp.start()
        return cp

    to_next, to_prev = (nxt * 2 + yl, tn), (prv * 2 + yl, tn)
    to_pair = (xc * 2 + 1 - yl, tn)
    big = (
        (hidden, rdd, rd_v, rd_o),
        (gum.at[:, 0], dgate, lg_v, lg_o),
        (gum.at[:, 1], dup, lu_v, lu_o),
    )

    def part(a, q, half):
        if a == 3:
            return part_in(summed_block(2 * q + yl, half)) + wyin[q, half].astype(F32)
        if a == 4:
            rows = pl.ds(pl.multiple_of(q % 2 * 256 + half * 128, 128), 128)
            return dot(rdm[q // 2, 0, rows, :], dy[0:HALF, :]) + dot(rdm[q // 2, 1, rows, :], dy[HALF:, :])
        rows = pl.ds(pl.multiple_of(q * 256 + half * 128, 128), 128)
        if a in (2, 5):
            cols = slice(0, 512) if a == 2 else slice(512, 1024)
            return dot(gum[0, 1, rows, :], dup[0, cols, :], NT) + dot(gum[1, 1, rows, :], dup[1, cols, :], NT)
        left, right = big[a][:2]

        def both(pick):
            return dot(left[0, rows, :], pick(0), NT) + dot(left[1, rows, :], pick(1), NT)

        if a == 0:
            return jnp.concatenate([both(lambda h, y=y: rdd[y, h]) for y in range(2)], axis=1)
        return both(lambda h: right[h])

    started = [[None] * 5 for _ in range(6)]
    steps = (p2, pn, pp, ysend, ra, rb, rc, rdn, ye)
    places = [tuple(ref.at[a] for ref in steps) for a in range(2)]

    def columns_of(a):
        at = pl.ds(0 if a == 2 else 512, 512)
        return tuple(ref.at[2, :, :, at] if ref.ndim == 4 else ref.at[2, :, at] for ref in steps)

    places.append(columns_of(2))
    for ref in (wring, lring):
        places.append(tuple(
            ref.at[at] if size == 1 else ref.at[pl.ds(at, size)]
            for at, size in ((0, 2), (2, 2), (4, 2), (6, 1), (7, 1), (8, 1), (9, 2), (11, 2), (13, 1))
        ))
    places.append(columns_of(5))

    crossed = []

    def cross_first():
        for n, q in enumerate((opp, nxt, prv, xc)):
            for half in range(2):
                wyout[q, half] = part_in(summed_block(2 * q + 1 - yl, half)).astype(BF)
            cp = pltpu.make_async_remote_copy(
                src_ref=wyout.at[q], dst_ref=wyin.at[q], send_sem=cross_send.at[n], recv_sem=cross_recv.at[n],
                device_id=to_pair, device_id_type=MESH,
            )
            cp.start()
            crossed.append(cp)

    def ring1(a):
        p2, _, _, _, ra, rb = places[a][:6]
        if a == 3:
            crossed[0].wait_recv()

        for half, (into, to) in enumerate(((ra, to_next), (rb, to_prev))):
            p2[half] = part(a, opp, half).astype(BF)
            started[a][half] = ship(p2.at[half], into, 5 * a + half, to)

    def ring2(a):
        _, pn, pp, _, ra, rb, rc, rdn, _ = places[a]
        if a == 3:
            crossed[1].wait_recv()
            crossed[2].wait_recv()

        def put_n(half):
            pn[half] = part(a, nxt, half).astype(BF)

        def put_p(half):
            pp[half] = part(a, prv, half).astype(BF)

        tiles(2, put_n)
        started[a][0].wait_recv()
        pn[0] = (pn[0].astype(F32) + ra[...].astype(F32)).astype(BF)
        started[a][2] = ship(pn, rc, 5 * a + 2, to_next)
        tiles(2, put_p)
        started[a][1].wait_recv()
        pp[1] = (pp[1].astype(F32) + rb[...].astype(F32)).astype(BF)
        started[a][3] = ship(pp, rdn, 5 * a + 3, to_prev)

    def kept(a, c):
        return c % 2, pl.ds((a * 2 + c // 2) * 128, 128)

    def ring3(a):
        _, _, _, ysend, _, _, rc, rdn, ye = places[a]
        if a == 3:
            crossed[3].wait_recv()
        started[a][2].wait_recv()
        started[a][3].wait_recv()

        def total(half):
            return part(a, xc, half) + rc[half].astype(F32) + rdn[half].astype(F32)

        if a == 3:
            for half in range(2):
                wsum[half * 128:(half + 1) * 128, :] = total(half).astype(BF)
            return
        ysend[...] = total(1 - yl).astype(BF)
        started[a][4] = ship(ysend, ye, 5 * a + 4, to_pair)
        own = total(yl)
        if a == 4:
            lown[...] = own
            return
        for c, cols in wide_columns(a):
            s, rows = kept(min(a, 2), c)
            upper[s, rows, :] = own[:, cols]

    def wide_columns(a):
        first = 2 if a == 5 else 0
        return [(first + c, slice(c * 256, (c + 1) * 256)) for c in range(2 if a in (2, 5) else 4)]

    def ring4(a):
        ye = places[a][8]
        started[a][4].wait_recv()
        if a == 4:
            ld_v[...] = (lown[...] + ye[...].astype(F32)).astype(BF)
            store(ld_v, ld_o.at[0])
            return
        out, out_h = big[min(a, 2)][2:]
        for c, cols in wide_columns(a):
            s, rows = kept(min(a, 2), c)
            out[:, c * 256:(c + 1) * 256] = (upper[s, rows, :] + ye[:, cols].astype(F32)).astype(BF)
        if a != 2:
            store(out, out_h.at[0])

    for h in range(2):
        await_bytes(ps.at[h], p_send.at[h])
    crossing = []

    def mids_over(gu, h):
        w, d = ((lg, dgate), (lu, dup))[gu]
        for q in range(2):
            src = pl.ds(pl.multiple_of((1 - yh) * 512 + q * 256, 256), 256)
            ps[gu, h, q * 256:(q + 1) * 256, :] = dot(w[src, :], d[h]).astype(BF)
        cp = pltpu.make_async_remote_copy(
            src_ref=ps.at[gu, h], dst_ref=back.at[yh, gu, h], send_sem=b_send.at[gu * 2 + h], recv_sem=b_recv.at[gu * 2 + h],
            device_id=(dp, over_y), device_id_type=MESH,
        )
        cp.start()
        crossing.append(cp)

    def mids_here(gu, h):
        w, d = ((lg, dgate), (lu, dup))[gu]
        for q in range(2):
            src = pl.ds(pl.multiple_of(yh * 512 + q * 256, 256), 256)
            back[yh, gu, h, q * 256:(q + 1) * 256, :] = dot(w[src, :], d[h]).astype(BF)

    ring1(0)
    backward(0)
    mids_over(0, 0)
    mids_over(1, 0)
    downs[0].wait_recv()
    relay(dm, rdm, m_send.at[2], m_recv.at[2], 0, 15, 0)
    backward(1)
    mids_over(0, 1)
    mids_over(1, 1)
    ring1(1)
    downs[1].wait_recv()
    relay(dm, rdm, m_send.at[3], m_recv.at[3], 0, 7, 1)
    ring1(2)
    ring1(5)
    mids_here(0, 0)
    mids_here(1, 0)
    ring2(0)
    mids_here(0, 1)
    mids_here(1, 1)
    ring2(1)

    def outputs():
        for h in range(2):
            await_bytes(rdm.at[:, h, pl.ds(0, 480)], m_recv.at[2 + h])
        ring1(4)
        for h in range(2):
            out_v[h * HALF:(h + 1) * HALF, :] = (
                dot(ldt[:, 0:512], rdm[0, h]) + dot(ldt[:, 512:], rdm[1, h])
            ).T.astype(BF)
        store(out_v, out_o)

    def stacked(h, b):
        rows = rows_at(b, KW)
        return jnp.concatenate([back[y, gu, h, rows, :] for y in range(2) for gu in range(2)], axis=0)

    def dx_part(h, zz, c):
        b = zz * 2 + c
        return dot(stacked(h, b), columns(b, 0, 1), TN)

    def for_sibling(h):
        for cp in crossing[2 * h:2 * h + 2]:
            cp.wait_recv()
        for d in range(8):
            zz = (z + 4 + d) % 8
            lgt[h * 8 + zz] = dx_part(h, zz, 1 - core).astype(BF)
            pltpu.make_async_remote_copy(
                src_ref=lgt.at[h * 8 + zz], dst_ref=sums_in.at[h, zz], send_sem=s_send.at[0], recv_sem=s_recv.at[h, d],
                device_id=(dp, sibling), device_id_type=MESH,
            ).start()

    def slab_sum(h, off):
        zz = (z + off) % 8
        await_bytes(sums_in.at[h, zz], s_recv.at[h, (off + 4) % 8])
        return dx_part(h, zz, core) + sums_in[h, zz].astype(F32)

    REACH = ((4, 3), (3, 4))
    links = []

    def chain(d, h):
        for way, (sign, to) in enumerate(((1, up_z), (-1, down_z))):
            far = REACH[h][way]
            if d > far:
                continue
            v = slab_sum(h, sign * d)
            if d < far:
                await_bytes(chain_in.at[h, way, d], ch_recv.at[h, way, d])
                v = v + chain_in[h, way, d].astype(F32)
            slot = (h * 2 + way) * 4 + d - 1
            lut[slot] = v.astype(BF)
            cp = pltpu.make_async_remote_copy(
                src_ref=lut.at[slot], dst_ref=chain_in.at[h, way, d - 1],
                send_sem=ch_send.at[slot], recv_sem=ch_recv.at[h, way, d - 1],
                device_id=(dp, to), device_id_type=MESH,
            )
            cp.start()
            links.append(cp)

    def part_in(b):
        return dot(stacked(0, b), xall[0, b]) + dot(stacked(1, b), xall[1, b])

    def tokens_grad(h):
        v = slab_sum(h, 0)
        for way in range(2):
            await_bytes(chain_in.at[h, way, 0], ch_recv.at[h, way, 0])
            v = v + chain_in[h, way, 0].astype(F32)
        dx_v[h * HALF:(h + 1) * HALF, :] = v.astype(BF)

    for_sibling(0)
    chain(4, 0)
    chain(3, 0)
    for_sibling(1)
    chain(4, 1)
    cross_first()
    chain(2, 0)
    relay(dm, rdm, m_send.at[3], m_recv.at[3], 7, 15, 1)
    ring1(3)
    ring2(2)
    ring3(0)
    chain(3, 1)
    ring2(3)
    outputs()
    ring2(5)
    chain(1, 0)
    ring3(1)
    chain(2, 1)

    ring3(3)
    final = []
    for par in range(2):
        for cs in range(2):
            to = (cs * 4 + ring // 4, yh * 16 + summed_block(dp, par))
            src, dst = wsum.at[pl.ds(par * 128 + cs * 64, 64)], wfin.at[ring % 4]
            away = pltpu.make_async_remote_copy(
                src_ref=src, dst_ref=dst, send_sem=wf_send.at[par * 2 + cs], recv_sem=wf_recv.at[0],
                device_id=to, device_id_type=MESH,
            )

            def keep(src=src, dst=dst):
                pltpu.make_async_copy(src, dst, wf_recv.at[0]).start()

            apart(*to, keep, away.start)
            final.append((to, away))
    ring3(2)
    ring2(4)
    tokens_grad(0)
    chain(1, 1)
    ring4(0)
    ring3(5)
    ring3(4)
    ring4(1)
    tokens_grad(1)
    store(dx_v, dx_o)
    ring4(2)
    ring4(5)
    await_bytes(wfin, wf_recv.at[0])
    for gu, (out, out_h) in enumerate(((rg_v, rg_o), (ru_v, ru_o))):
        out[...] = jnp.concatenate([wfin[j, gu * KW:(gu + 1) * KW, :] for j in range(4)], axis=0).T
        store(out, out_h.at[0])
    ring4(4)

    for h in range(2):
        await_bytes(xall.at[h, pl.ds(0, 15)], x_send.at[h])
    to_y.wait_send()
    await_bytes(rdd.at[:, :, pl.ds(0, 480)], d_send.at[1])
    await_bytes(wp.at[0, pl.ds(0, 15)], w_send.at[0])
    await_bytes(wp.at[pl.ds(0, 3)], w_send.at[1])
    for h in range(2):
        await_bytes(rdm.at[:, h, pl.ds(0, 480)], m_send.at[2 + h])
    for cp in crossing + links + downs:
        cp.wait_send()
    await_bytes(sums_in, s_send.at[0])
    for group in started + [crossed]:
        for cp in group:
            if cp is not None:
                cp.wait_send()
    for to, away in final:
        apart(*to, lambda: None, away.wait_send)
    for cp in stores:
        cp.wait()


def hand_over(*refs):
    src, dst, held, (sem,) = refs[:8], refs[8:16], refs[16:24], refs[24:]
    arriving = [pltpu.make_async_copy(src[i], held[i], sem.at[0, i]) for i in range(8)]
    leaving = [pltpu.make_async_copy(held[i], dst[i], sem.at[1, i]) for i in range(8)]
    for cp in arriving:
        cp.start()
    for i in range(8):
        arriving[i].wait()
        leaving[i].start()
    for cp in leaving:
        cp.wait()


def per_device(tokens, gate_in, gate_out, up_in, up_out, down_in, down_out, cotangent):
    anyw = pl.BlockSpec(memory_space=pl.ANY)
    out_shape = (
        jax.ShapeDtypeStruct((TOK, DB), BF),
        jax.ShapeDtypeStruct((TOK, DB), BF),
        jax.ShapeDtypeStruct((1, DB, 128), BF),
        jax.ShapeDtypeStruct((1, 128, MB), BF),
        jax.ShapeDtypeStruct((1, DB, 128), BF),
        jax.ShapeDtypeStruct((1, 128, MB), BF),
        jax.ShapeDtypeStruct((1, 128, MB), BF),
        jax.ShapeDtypeStruct((1, 128, DB), BF),
    )
    V = pltpu.VMEM
    mids = V((2, MB, HALF), BF)
    wide = V((2, MB, HALF), F32)
    square = V((MB, MB), BF)
    dma = pltpu.SemaphoreType.DMA
    scratch = [
        V((TOK, DB), BF), V((TOK, DB), BF), V((DB, 128), BF), V((128, MB), BF),
        V((DB, 128), BF), V((128, MB), BF), V((128, MB), BF), V((128, DB), BF),
        V((2, 16, HALF, DB), BF), V((2, 512, DB), BF), V((4, 16, 2, 16, DB), BF), V((2, 2, 512, HALF), BF),
        V((DB, MB), BF), square, V((DB, MB), BF), square, square, V((MB, DB), BF), V((TOK, DB), BF),
        V((16, 256, 256), BF), V((16, 256, 256), BF), square, V((DB, MB), BF),
        V((2, 512, HALF), BF), V((2, 2, 512, HALF), BF), V((2, 2, 512, HALF), BF),
        V((2, 512, HALF), BF), V((2, 2, 512, HALF), BF), V((2, 2, 512, HALF), BF), V((2, 2, MB, HALF), BF),
        V((2, 2, 2, 512, HALF), BF), V((2, 8, HALF, DB), BF), V((2, 2, 4, HALF, DB), BF),
        wide, wide, mids, mids, mids,
        V((3, 2, 128, MB), BF), V((3, 2, 128, MB), BF), V((3, 2, 128, MB), BF), V((3, 128, MB), BF),
        V((3, 128, MB), BF), V((3, 128, MB), BF), V((3, 2, 128, MB), BF), V((3, 2, 128, MB), BF), V((3, 128, MB), BF),
        V((14, 128, DB), BF), V((14, 128, DB), BF), V((4, 2, 128, DB), BF), V((4, 2, 128, DB), BF),
        V((128, DB), F32), V((256, DB), BF), V((4, 64, DB), BF),
        dma((9,)), dma((8,)), dma((2,)), dma((2, 8)), dma((2, 8)), dma((2,)), dma((2,)), dma((2,)), dma((2,)),
        dma((2,)), dma((2,)),
        dma((4,)), dma((4,)), dma((30,)), dma((30,)), dma((4,)), dma((4,)),
        dma((4,)), dma((4,)), dma((1,)), dma((2, 8)), dma((16,)), dma((2, 2, 4)), dma((4,)), dma((1,)),
    ]
    results = pl.pallas_call(
        kernel,
        out_shape=out_shape,
        in_specs=[anyw] * 8,
        out_specs=(anyw,) * 8,
        scratch_shapes=scratch,
        compiler_params=pltpu.CompilerParams(
            collective_id=0, has_side_effects=True, vmem_limit_bytes=62 * 2**20
        ),
        cost_estimate=pl.CostEstimate(flops=12_000_000_000, bytes_accessed=10_000_000, transcendentals=1_000_000),
    )(tokens, gate_in, gate_out, up_in, up_out, down_in, down_out, cotangent)
    return pl.pallas_call(
        hand_over,
        out_shape=out_shape,
        in_specs=[anyw] * 8,
        out_specs=(anyw,) * 8,
        scratch_shapes=[V(o.shape, BF) for o in out_shape] + [pltpu.SemaphoreType.DMA((2, 8))],
    )(*results)


def solution(mesh):
    in_specs = (
        P("dp", "tensor"),
        P("tensor", None, None),
        P("tensor", None, None),
        P("tensor", None, None),
        P("tensor", None, None),
        P("tensor", None, None),
        P("tensor", None, None),
        P("dp", "tensor"),
    )
    out_specs = (
        P("dp", "tensor"),
        P("dp", "tensor"),
        P("tensor", None, "dp"),
        P("tensor", "dp", None),
        P("tensor", None, "dp"),
        P("tensor", "dp", None),
        P("tensor", "dp", None),
        P("tensor", "dp", None),
    )
    return jax.shard_map(
        per_device, mesh=mesh, in_specs=in_specs, out_specs=out_specs, check_vma=False
    )
```
